32 devices in a mesh: head: 8 (over z, x), ctx: 2 (over y), dp: 2 (over core).
Axes of the slice: x: 2, y: 2, z: 4, core: 2. Of those that a mesh axis runs over, the one named last changes fastest.
Arguments:
- query_nope: bfloat16 [2, 256, 128, 128], P('dp', 'ctx', 'head'), may hold values from -6 to 6
- query_rope: bfloat16 [2, 256, 128, 64], P('dp', 'ctx', 'head'), may hold values from -10 to 10
- query_pos: int32 [2, 256], P('dp', 'ctx'), may hold values from 64 to 255
- latent_cache: bfloat16 [2, 4, 64, 576], P('dp', 'ctx'), may hold values from -6 to 6
- block_table: int32 [2, 4], P('dp'), may hold values from 0 to 3, each once within a row
- key_up: bfloat16 [128, 128, 512], P('head'), may hold values from -0.5 to 0.5
- value_up: bfloat16 [128, 512, 128], P('head'), may hold values from -0.25 to 0.25
- grad_out: bfloat16 [2, 256, 128, 128], P('dp', 'ctx', 'head'), may hold values from -6 to 6
Outputs:
- grad_query_nope: float32 [2, 256, 128, 128], P('dp', 'ctx', 'head')
- grad_query_rope: float32 [2, 256, 128, 64], P('dp', 'ctx', 'head')
- grad_cache: float32 [2, 4, 64, 576], P('dp', 'ctx')
- grad_key_up: float32 [128, 128, 512], P('head', ('ctx', 'dp'))
- grad_value_up: float32 [128, 512, 128], P('head', ('ctx', 'dp'))
The draws below stay inside these ranges and needn't reach their ends.
Inputs may be any that keep to these rules, and one draw needn't show every extreme that they name: Each row is a permutation: logical block b of sequence s lies in physical block block_table[s, b].
All inputs are finite; a program needn't handle non-finite values.
Results may differ from the reference program's by a relative error of at most 0.025.
Values may be sent and summed in bfloat16 or wider, within the bound.
No kernel may reach another device: no remote copies, remote signals or barrier semaphores. Data moves between devices by JAX's collectives and lax.ppermute only.
A program may use at most 64 MiB of HBM per device.

```python
import jax
import jax.numpy as jnp
from jax import lax

H = 128
DNOPE = 128
LAT = 512
ROPE = 64
DV = 128
PAGE = 64
Q_DEV = 128
SEQS = 2
Q = 256
BLOCKS = 4
KEYS = 256
N_CTX = 2


def draw_query_rope(key, part):
    full_shape = (SEQS, Q, H, ROPE)
    drawn = jnp.clip(jax.random.normal(jax.random.fold_in(key, 11), full_shape, jnp.float32), -4.0, 4.0)
    return drawn.astype(jnp.bfloat16)


def draw_latent_cache(key, part):
    full_shape = (SEQS, BLOCKS, PAGE, LAT + ROPE)
    drawn = jnp.clip(jax.random.normal(jax.random.fold_in(key, 23), full_shape, jnp.float32), -4.0, 4.0)
    return drawn.astype(jnp.bfloat16)


def place_ends(values, rng, low, largest):
    dims = values.shape
    place = [jax.random.randint(jax.random.fold_in(rng, axis), (), 0, dims[axis]) for axis in range(len(dims))]
    values = values.at[tuple(place)].set(low)
    longest = dims.index(max(dims))
    place[longest] = (place[longest] + 1) % dims[longest]
    return values.at[tuple(place)].set(largest)


def block_scale(stream_key, dims, cuts, least, largest):
    level = 1.0
    for axis_at, shards_of in cuts:
        draws = jax.random.uniform(jax.random.fold_in(jax.random.fold_in(stream_key, 6), axis_at), (shards_of,), jnp.float32, least / len(cuts), largest / len(cuts))
        level = level * jnp.repeat(jnp.exp(draws), dims[axis_at] // shards_of).reshape((-1,) + (1,) * (len(dims) - 1 - axis_at))
    return level


def scatter_about(rng, dims, spread, limit, pieces=(), kind=jnp.bfloat16):
    values = jax.random.normal(rng, dims, jnp.float32) * spread
    if len(pieces) > 0:
        values = block_scale(rng, dims, pieces, -0.22, 0.18) * values
    return jnp.clip(values, min=-limit, max=limit).astype(kind)


def setup_inputs(seed: int = 0) -> dict:
    splits = jax.random.split(jax.random.key(seed), 9)
    return {
        "query_nope": scatter_about(splits[0], (SEQS, Q, H, DNOPE), 1.0, 6.0, ((0, 2), (1, 2), (2, 8))),
        "query_rope": draw_query_rope(jax.random.fold_in(splits[8], 71), 0),
        "query_pos": place_ends(jax.random.randint(splits[2], (SEQS, Q), PAGE, KEYS), jax.random.fold_in(splits[2], 1), PAGE, KEYS - 1).astype(jnp.int32),
        "latent_cache": draw_latent_cache(jax.random.fold_in(splits[8], 71), 0),
        "block_table": jax.vmap(lambda own: jax.random.permutation(own, BLOCKS))(jax.random.split(splits[4], SEQS)).reshape((SEQS, BLOCKS)).astype(jnp.int32),
        "key_up": scatter_about(splits[5], (H, DNOPE, LAT), DNOPE ** -0.5, 0.5, ((0, 8),)),
        "value_up": scatter_about(splits[6], (H, LAT, DV), LAT ** -0.5, 0.25, ((0, 8),)),
        "grad_out": scatter_about(splits[7], (SEQS, Q, H, DV), 1.0, 6.0, ((0, 2), (1, 2), (2, 8))),
    }


softmax_scale = 192.0 ** -0.5


def head_terms(key_rows, key_pos, query_position, nope_rows, rope_rows, key_map, value_map, out_grad):
    query_latent = jnp.dot(nope_rows, key_map, preferred_element_type=jnp.float32).astype(jnp.bfloat16)
    query_rows = jnp.concatenate([query_latent, rope_rows], axis=1)
    scores = jnp.dot(query_rows, key_rows.T, preferred_element_type=jnp.float32) * softmax_scale
    visible = key_pos[None, :] <= query_position[:, None]
    scores = jnp.where(visible, scores, -jnp.inf)
    row_max = jnp.max(scores, axis=1, keepdims=True)
    weights = jnp.exp(scores - row_max)
    attn_probs = weights / jnp.sum(weights, axis=1, keepdims=True)
    probs_b = attn_probs.astype(jnp.bfloat16)
    value_rows = key_rows[:, :LAT]
    attn_out = jnp.dot(probs_b, value_rows, preferred_element_type=jnp.float32).astype(jnp.bfloat16)
    grad_latent = jnp.dot(out_grad, value_map.T, preferred_element_type=jnp.float32).astype(jnp.bfloat16)
    grad_probs = jnp.dot(grad_latent, value_rows.T, preferred_element_type=jnp.float32)
    row_delta = jnp.sum(attn_probs * grad_probs, axis=1, keepdims=True)
    grad_scores = (attn_probs * (grad_probs - row_delta) * softmax_scale).astype(jnp.bfloat16)
    grad_query = jnp.dot(grad_scores, key_rows, preferred_element_type=jnp.float32)
    grad_rope = grad_query[:, LAT:]
    grad_qlatent = grad_query[:, :LAT].astype(jnp.bfloat16)
    grad_nope = jnp.dot(grad_qlatent, key_map.T, preferred_element_type=jnp.float32)
    nope_blocks = nope_rows.astype(jnp.float32).reshape(N_CTX, Q_DEV, DNOPE)
    qlat_blocks = grad_qlatent.astype(jnp.float32).reshape(N_CTX, Q_DEV, LAT)
    key_part = jnp.einsum("bqn,bql->bnl", nope_blocks, qlat_blocks).astype(jnp.bfloat16)
    out_blocks = attn_out.astype(jnp.float32).reshape(N_CTX, Q_DEV, LAT)
    grad_blocks = out_grad.astype(jnp.float32).reshape(N_CTX, Q_DEV, DV)
    value_part = jnp.einsum("bql,bqv->blv", out_blocks, grad_blocks).astype(jnp.bfloat16)
    key_part = lax.optimization_barrier(key_part)
    value_part = lax.optimization_barrier(value_part)
    grad_keys = jnp.dot(grad_scores.T, query_rows, preferred_element_type=jnp.float32)
    grad_values = jnp.dot(probs_b.T, grad_latent, preferred_element_type=jnp.float32)
    grad_keys = grad_keys + jnp.pad(grad_values, ((0, 0), (0, ROPE)))
    key_total = jnp.sum(key_part.astype(jnp.float32), axis=0)
    value_total = jnp.sum(value_part.astype(jnp.float32), axis=0)
    return grad_nope, grad_rope, key_total, value_total, grad_keys


def reference(query_nope, query_rope, query_pos, latent_cache, block_table, key_up, value_up, grad_out):
    nope_list, rope_list, cache_list = [], [], []
    key_total = jnp.zeros((H, DNOPE, LAT), jnp.float32)
    value_total = jnp.zeros((H, LAT, DV), jnp.float32)
    key_pos = jnp.arange(KEYS, dtype=jnp.int32)
    for sequence in range(SEQS):
        slot_table = block_table[sequence].astype(jnp.int32)
        key_rows = latent_cache[sequence][slot_table].reshape(KEYS, LAT + ROPE)
        query_position = query_pos[sequence]

        def head_step(running, head_inputs):
            nope_rows, rope_rows, key_map, value_map, out_grad = head_inputs
            grad_nope, grad_rope, key_part, value_part, grad_keys = head_terms(
                key_rows, key_pos, query_position, nope_rows, rope_rows, key_map, value_map, out_grad)
            return running + grad_keys, (grad_nope, grad_rope, key_part, value_part)

        head_inputs = (jnp.swapaxes(query_nope[sequence], 0, 1), jnp.swapaxes(query_rope[sequence], 0, 1),
                       key_up, value_up, jnp.swapaxes(grad_out[sequence], 0, 1))
        grad_keys, (grad_nope, grad_rope, key_part, value_part) = lax.scan(
            head_step, jnp.zeros((KEYS, LAT + ROPE), jnp.float32), head_inputs)
        physical = jnp.zeros((BLOCKS, PAGE, LAT + ROPE), jnp.float32)
        physical = physical.at[slot_table].set(grad_keys.reshape(BLOCKS, PAGE, LAT + ROPE))
        nope_list.append(jnp.swapaxes(grad_nope, 0, 1))
        rope_list.append(jnp.swapaxes(grad_rope, 0, 1))
        cache_list.append(physical)
        key_total = key_total + key_part
        value_total = value_total + value_part
    return (jnp.stack(nope_list), jnp.stack(rope_list), jnp.stack(cache_list), key_total, value_total)
```

```python
import functools

import jax
import jax.numpy as jnp
from jax import lax
from jax.experimental import pallas as pl
from jax.experimental.pallas import tpu as pltpu
from jax.sharding import PartitionSpec as P

softmax_scale = 192.0 ** (-0.5)
F32 = jnp.float32
BF16 = jnp.bfloat16
VMEM_LIMIT = 56 * 1024 * 1024


def dot_nn(a, b):
    return lax.dot_general(a, b, (((1,), (0,)), ((), ())), preferred_element_type=F32)


def dot_nt(a, b):
    return lax.dot_general(a, b, (((1,), (1,)), ((), ())), preferred_element_type=F32)


def dot_tn(a, b):
    return lax.dot_general(a, b, (((0,), (0,)), ((), ())), preferred_element_type=F32)


def main_kernel(
    paired, page_rows, latent_width,
    place_ref, table_ref, pos_ref, keys_ref, qcat_ref, qt_ref, go_ref, ku_ref, vu_ref,
    ds_ref, kn_ref, *rest,
):
    if paired:
        keep0, keep1, send0, send1, mine_ref, other_ref, vt_ref, bp_ref, acc_ref = rest
    else:
        wk_ref, wv_ref, all_ref, vt_ref, bp_ref, acc_ref = rest
    heads, nope_width = ku_ref.shape[0], ku_ref.shape[1]
    value_width = vu_ref.shape[2]
    key_count, row_width = keys_ref.shape
    query_count = go_ref.shape[1]
    blocks = table_ref.shape[0]
    step = pl.program_id(0)
    last = pl.num_programs(0) - 1
    latent = keys_ref[:, :latent_width]
    rotary = keys_ref[:, latent_width:]
    nope_slice, value_slice = bp_ref.shape[1] // heads, vt_ref.shape[1]
    slices = vt_ref.shape[0]

    def place_of(s):
        if not paired:
            return s
        return jnp.bitwise_xor(s % 2, place_ref[1]) * 2 + jnp.bitwise_xor(s // 2, place_ref[0])

    @pl.when(step == 0)
    def _():
        acc_ref[...] = jnp.zeros_like(acc_ref)
        turned = jnp.transpose(latent.astype(F32)).astype(BF16)
        for s in range(slices):
            vt_ref[place_of(s)] = turned[s * value_slice:(s + 1) * value_slice]

    row = lax.broadcasted_iota(jnp.int32, (page_rows, query_count), 0)
    positions = []
    for slot in range(blocks):
        logical = jnp.int32(0)
        for b in range(blocks):
            logical = logical + jnp.where(table_ref[b] == slot, b, 0)
        positions.append(row + logical * page_rows)
    visible = jnp.concatenate(positions, axis=0) <= pos_ref[...]

    kn = dot_nt(latent, ku_ref[...].reshape(heads * nope_width, latent_width)).astype(BF16)
    vu = jnp.concatenate([vu_ref[h] for h in range(heads)], axis=1)
    values = dot_nn(latent, vu).astype(BF16)
    gkn_all, gv_all = [], []
    rotary_sum = None
    for h in range(heads):
        kn_h = kn[:, h * nope_width:(h + 1) * nope_width]
        kn_ref[h] = kn_h
        kcat = jnp.concatenate([kn_h, rotary], axis=1)
        qcat = qcat_ref[h]
        scores = dot_nt(kcat, qcat) * softmax_scale
        scores = jnp.where(visible, scores, -jnp.inf)
        grad_probs = dot_nt(values[:, h * value_width:(h + 1) * value_width], go_ref[h])
        top = jnp.max(scores, axis=0, keepdims=True)
        weights = jnp.exp(scores - top)
        inverse = 1.0 / jnp.sum(weights, axis=0, keepdims=True)
        probs = weights * inverse
        delta = jnp.sum(probs * grad_probs, axis=0, keepdims=True)
        ds = (probs * (grad_probs - delta) * softmax_scale).astype(BF16)
        ds_ref[h] = ds
        gk = dot_nn(ds, qcat)
        gkn_all.append(gk[:, :nope_width].astype(BF16))
        rotary_sum = gk[:, nope_width:] if rotary_sum is None else rotary_sum + gk[:, nope_width:]
        gv_all.append(dot_nn(probs.astype(BF16), go_ref[h]).astype(BF16))
        b = dot_nt(qt_ref[h], ds).astype(BF16)
        for s in range(slices):
            bp_ref[place_of(s), h * nope_slice:(h + 1) * nope_slice] = b[s * nope_slice:(s + 1) * nope_slice]
    gkn = jnp.concatenate(gkn_all, axis=1)
    gv = jnp.concatenate(gv_all, axis=1)
    acc_ref[:, :latent_width] += dot_nn(gkn, ku_ref[...].reshape(heads * nope_width, latent_width)) + dot_nt(gv, vu)
    acc_ref[:, latent_width:] += rotary_sum
    outs = (keep0, keep1, send0, send1) if paired else (None,) * slices
    for s in range(slices):
        key_part = dot_nn(bp_ref[s], latent).astype(BF16)
        value_part = dot_nn(vt_ref[s], gv).astype(BF16)
        for h in range(heads):
            rows = key_part[h * nope_slice:(h + 1) * nope_slice]
            columns = value_part[:, h * value_width:(h + 1) * value_width]
            if paired:
                for j in range(latent_width // value_width):
                    outs[s][h, 0, j * nope_slice:(j + 1) * nope_slice] = rows[:, j * value_width:(j + 1) * value_width]
                outs[s][h, 1] = columns
            else:
                wk_ref[h, s * nope_slice:(s + 1) * nope_slice] = rows
                wv_ref[h, s * value_slice:(s + 1) * value_slice] = columns

    @pl.when(step == last)
    def _():
        if paired:
            half = key_count // 2
            begin = pl.multiple_of(place_ref[0] * half, half)
            away = pl.multiple_of((1 - place_ref[0]) * half, half)
            mine_ref[...] = acc_ref[pl.ds(begin, half)].astype(BF16)
            other_ref[...] = acc_ref[pl.ds(away, half)].astype(BF16)
        else:
            all_ref[...] = acc_ref[...].astype(BF16)


def attention_backward(paired, place, table, pos, keys, qcat, qt, go, key_up, value_up, page_rows, group):
    heads, nope_width, latent_width = key_up.shape
    value_width = value_up.shape[2]
    query_count = go.shape[1]
    key_count, row_width = keys.shape
    slices = 4 if paired else 1
    by_head = lambda *dims: pl.BlockSpec((group,) + dims, lambda i: (i,) + (0,) * len(dims))
    whole = lambda *dims: pl.BlockSpec(dims, lambda i: (0,) * len(dims))
    smem = pl.BlockSpec(memory_space=pltpu.SMEM)
    out = lambda *dims: jax.ShapeDtypeStruct(dims, BF16)
    shapes = [out(heads, key_count, query_count), out(heads, key_count, nope_width)]
    specs = [by_head(key_count, query_count), by_head(key_count, nope_width)]
    if paired:
        depth = latent_width // slices
        shapes += [out(heads, 2, depth, value_width)] * 4 + [out(key_count // 2, row_width)] * 2
        specs += [by_head(2, depth, value_width)] * 4 + [whole(key_count // 2, row_width)] * 2
    else:
        shapes += [out(heads, nope_width, latent_width), out(heads, latent_width, value_width), out(key_count, row_width)]
        specs += [by_head(nope_width, latent_width), by_head(latent_width, value_width), whole(key_count, row_width)]
    return pl.pallas_call(
        functools.partial(main_kernel, paired, page_rows, latent_width),
        grid=(heads // group,),
        in_specs=[
            smem, smem, whole(1, query_count), whole(key_count, row_width),
            by_head(query_count, qcat.shape[2]), by_head(nope_width, query_count), by_head(query_count, value_width),
            by_head(nope_width, latent_width), by_head(latent_width, value_width),
        ],
        out_specs=specs,
        out_shape=shapes,
        scratch_shapes=[
            pltpu.VMEM((slices, latent_width // slices, key_count), BF16),
            pltpu.VMEM((slices, group * nope_width // slices, key_count), BF16),
            pltpu.VMEM((key_count, row_width), F32),
        ],
        compiler_params=pltpu.CompilerParams(vmem_limit_bytes=VMEM_LIMIT),
        cost_estimate=pl.CostEstimate(flops=6_000_000_000, bytes_accessed=12_000_000, transcendentals=0),
        name="attention_backward",
    )(place, table, pos, keys, qcat, qt, go, key_up, value_up)


def query_kernel(ds_ref, kn_ref, rotary_ref, nope_ref, rope_ref):
    nope_width = kn_ref.shape[2]
    heads = ds_ref.shape[0]
    query_count = ds_ref.shape[2]
    rotary = rotary_ref[...]
    for h in range(heads):
        kcat = jnp.concatenate([kn_ref[h], rotary], axis=1)
        gq = dot_tn(ds_ref[h], kcat)
        nope_ref[pl.ds(h, query_count, stride=heads), :] = gq[:, :nope_width]
        rope_ref[pl.ds(h, query_count, stride=heads), :] = gq[:, nope_width:]


def query_gradient(ds, kn, rotary):
    heads, key_count, query_count = ds.shape
    nope_width, rope_width = kn.shape[2], rotary.shape[1]
    nope, rope = pl.pallas_call(
        query_kernel,
        out_shape=[
            jax.ShapeDtypeStruct((query_count * heads, nope_width), F32),
            jax.ShapeDtypeStruct((query_count * heads, rope_width), F32),
        ],
        compiler_params=pltpu.CompilerParams(vmem_limit_bytes=VMEM_LIMIT),
        cost_estimate=pl.CostEstimate(flops=1_000_000_000, bytes_accessed=5_000_000, transcendentals=0),
        name="query_gradient",
    )(ds, kn, rotary)
    return nope.reshape(1, query_count, heads, nope_width), rope.reshape(1, query_count, heads, rope_width)


def finish_kernel(own_ref, near_ref, far_ref, key_ref, value_ref):
    rows = key_ref.shape[1]
    width = own_ref.shape[3]
    for h in range(key_ref.shape[0]):
        total = own_ref[h].astype(F32) + near_ref[h].astype(F32) + far_ref[h].astype(F32)
        for j in range(key_ref.shape[2] // width):
            key_ref[h, :, j * width:(j + 1) * width] = total[0, j * rows:(j + 1) * rows]
        value_ref[h] = total[1]


def finish(own, near, far, group):
    heads, _, depth, width = own.shape
    rows = depth // 4
    return pl.pallas_call(
        finish_kernel,
        grid=(heads // group,),
        in_specs=[pl.BlockSpec((group, 2, depth, width), lambda i: (i, 0, 0, 0))] * 3,
        out_specs=[
            pl.BlockSpec((group, rows, 4 * width), lambda i: (i, 0, 0)),
            pl.BlockSpec((group, depth, width), lambda i: (i, 0, 0)),
        ],
        out_shape=[
            jax.ShapeDtypeStruct((heads, rows, 4 * width), F32),
            jax.ShapeDtypeStruct((heads, depth, width), F32),
        ],
        compiler_params=pltpu.CompilerParams(vmem_limit_bytes=VMEM_LIMIT),
        name="finish",
    )(own, near, far)


def swap(x, axis, size, bits):
    return lax.ppermute(x, axis, [(i, i ^ bits) for i in range(size)])


def on_device(
    sizes, query_nope, query_rope, query_pos, latent_cache, block_table, key_up, value_up, grad_out
):
    head_size, ctx_size, dp_size = sizes
    heads, nope_width, latent_width = key_up.shape
    value_width = value_up.shape[2]
    page_rows, row_width = latent_cache.shape[2:]
    paired = (
        ctx_size == 2 and dp_size == 2 and latent_width == 4 * value_width and nope_width == value_width
        and nope_width % 64 == 0 and value_width % 128 == 0 and heads % 8 == 0
    )
    own_rows = latent_cache[0].reshape(-1, row_width)
    if ctx_size == 2:
        other_rows = swap(own_rows, "ctx", 2, 1)
        first = lax.axis_index("ctx") == 0
        keys = jnp.concatenate(
            [jnp.where(first, own_rows, other_rows), jnp.where(first, other_rows, own_rows)], axis=0
        )
    else:
        keys = lax.all_gather(own_rows, "ctx", axis=0, tiled=True)
    qcat = jnp.swapaxes(jnp.concatenate([query_nope[0], query_rope[0]], axis=2), 0, 1)
    qt = jnp.transpose(query_nope[0], (1, 2, 0))
    go = jnp.swapaxes(grad_out[0], 0, 1)
    place = jnp.stack([lax.axis_index("ctx"), lax.axis_index("dp")]).astype(jnp.int32)
    group = 4 if heads % 4 == 0 else 1
    results = attention_backward(
        paired, place, block_table[0], query_pos, keys, qcat, qt, go, key_up, value_up, page_rows, group
    )
    ds, kn = results[:2]
    rotary = keys[:, latent_width:]
    if heads % 8 == 0:
        grad_nope, grad_rope = query_gradient(ds, kn, rotary)
    else:
        grad_nope = jnp.einsum("hkq,hkn->qhn", ds, kn, preferred_element_type=F32)[None]
        grad_rope = jnp.einsum("hkq,kr->qhr", ds, rotary, preferred_element_type=F32)[None]

    if paired:
        keep0, keep1, send0, send1, mine, other = results[2:]
        near1 = swap(send1, "dp", 2, 1)
        share = mine.astype(F32) + swap(other, "ctx", 2, 1).astype(F32)
        near0 = swap(send0, "dp", 2, 1)
        far = swap((keep1.astype(F32) + near1.astype(F32)).astype(BF16), "ctx", 2, 1)
    else:
        wk, wv, rows = results[2:]
        grad_key_map = lax.psum_scatter(wk, ("ctx", "dp"), scatter_dimension=1, tiled=True).astype(F32)
        grad_value_map = lax.psum_scatter(wv, ("ctx", "dp"), scatter_dimension=1, tiled=True).astype(F32)
        share = lax.psum_scatter(rows, "ctx", scatter_dimension=0, tiled=True).astype(F32)
    if head_size & (head_size - 1) == 0:
        bits = 1
        while bits < head_size:
            rounded = share.astype(BF16)
            got = swap(rounded, "head", head_size, bits | (bits >> 1) if bits >= 4 else bits)
            share = rounded.astype(F32) + got.astype(F32)
            bits *= 2
    else:
        share = lax.psum(share.astype(BF16), "head").astype(F32)
    if paired:
        grad_key_map, grad_value_map = finish(keep0, near0, far, 4)
    return (
        grad_nope,
        grad_rope,
        share.reshape(latent_cache.shape),
        grad_key_map,
        grad_value_map,
    )


def solution(mesh):
    sizes = tuple(mesh.shape[axis] for axis in ("head", "ctx", "dp"))
    placed = (
        P("dp", "ctx", "head", None),
        P("dp", "ctx", "head", None),
        P("dp", "ctx"),
        P("dp", "ctx", None, None),
        P("dp", None),
        P("head", None, None),
        P("head", None, None),
        P("dp", "ctx", "head", None),
    )
    return jax.shard_map(
        functools.partial(on_device, sizes),
        mesh=mesh,
        in_specs=placed,
        out_specs=(
            P("dp", "ctx", "head", None),
            P("dp", "ctx", "head", None),
            P("dp", "ctx", None, None),
            P("head", ("ctx", "dp"), None),
            P("head", ("ctx", "dp"), None),
        ),
        check_vma=False,
    )
```

```python
import functools

import jax
import jax.numpy as jnp
from jax import lax
from jax.experimental import pallas as pl
from jax.experimental.pallas import tpu as pltpu
from jax.sharding import PartitionSpec as P

softmax_scale = 192.0 ** (-0.5)
F32 = jnp.float32
BF16 = jnp.bfloat16
MIB = 1024 * 1024
PLAN = ((4, True), (4, True), (8, False))


def dot_nn(a, b):
    return lax.dot_general(a, b, (((1,), (0,)), ((), ())), preferred_element_type=F32)


def dot_nt(a, b):
    return lax.dot_general(a, b, (((1,), (1,)), ((), ())), preferred_element_type=F32)


def dot_tn(a, b):
    return lax.dot_general(a, b, (((0,), (0,)), ((), ())), preferred_element_type=F32)


def params(mib):
    return pltpu.CompilerParams(vmem_limit_bytes=mib * MIB)


def cost(flops, moved):
    return pl.CostEstimate(flops=flops, bytes_accessed=moved, transcendentals=0)


def prepare_kernel(
    parts, page_rows, nope_hbm, rope_hbm, go_hbm, ku_hbm, vu_hbm, own_hbm, pos_hbm, table_hbm,
    qt_ref, go_ref, ku_ref, vu_ref, own_ref, bias_ref, kn_ref, va_ref,
    nope_in, go_in, rows_ref, pos_ref, table_ref, sems,
):
    heads, nope_width, latent_width = ku_ref.shape
    value_width = vu_ref.shape[2]
    query_count = go_ref.shape[1]
    moves = (
        (nope_hbm, nope_in), (go_hbm, go_in), (own_hbm, own_ref), (ku_hbm, ku_ref), (vu_hbm, vu_ref),
        (rope_hbm, qt_ref.at[:, nope_width:, :]), (table_hbm, table_ref), (pos_hbm, pos_ref),
    )
    copies = [pltpu.make_async_copy(a, b, sems.at[i]) for i, (a, b) in enumerate(moves)]
    for copy in copies:
        copy.start()
    copies[0].wait()
    rows_ref[...] = nope_in[...].astype(F32).reshape(query_count * heads, nope_width)
    for h in range(heads):
        qt_ref[h, :nope_width] = jnp.transpose(rows_ref[pl.ds(h, query_count, stride=heads), :]).astype(BF16)
    copies[1].wait()
    rows_ref[...] = go_in[...].astype(F32).reshape(query_count * heads, nope_width)
    for h in range(heads):
        go_ref[h] = rows_ref[pl.ds(h, query_count, stride=heads), :].astype(BF16)
    copies[6].wait()
    copies[7].wait()
    blocks = table_ref.shape[1]
    row = lax.broadcasted_iota(jnp.int32, (page_rows, query_count), 0)
    part_blocks = blocks // parts
    for i in range(blocks):
        slot = jnp.bitwise_xor(lax.axis_index("ctx"), i // part_blocks) * part_blocks + i % part_blocks if parts == 2 else i
        logical = jnp.int32(0)
        for b in range(blocks):
            logical = logical + jnp.where(table_ref[0, b] == slot, b, 0)
        visible = row + logical * page_rows <= pos_ref[...]
        bias_ref[i * page_rows:(i + 1) * page_rows] = jnp.where(visible, 0.0, -jnp.inf)
    copies[2].wait()
    latent = own_ref[:, :latent_width]
    copies[3].wait()
    step = 2
    for h in range(0, heads, step):
        ku = ku_ref[h:h + step].reshape(step * nope_width, latent_width)
        kn_ref[:, h * nope_width:(h + step) * nope_width] = dot_nt(latent, ku).astype(BF16)
    copies[4].wait()
    for h in range(0, heads, step):
        vu = jnp.concatenate([vu_ref[h + i] for i in range(step)], axis=1)
        va_ref[:, h * value_width:(h + step) * value_width] = dot_nn(latent, vu).astype(BF16)
    copies[5].wait()


def prepare(parts, nope, rope, go, key_up, value_up, own, pos, table, page_rows):
    query_count, heads, nope_width = nope.shape
    value_width = go.shape[2]
    key_count = table.shape[1] * page_rows
    out = lambda *dims: jax.ShapeDtypeStruct(dims, BF16)
    hbm = pl.BlockSpec(memory_space=pltpu.HBM)
    return pl.pallas_call(
        functools.partial(prepare_kernel, parts, page_rows),
        in_specs=[hbm] * 8,
        out_specs=[pl.BlockSpec(memory_space=pltpu.VMEM)] * 8,
        out_shape=[
            out(heads, nope_width + rope.shape[1], query_count), out(heads, query_count, value_width),
            out(*key_up.shape), out(*value_up.shape), out(*own.shape),
            jax.ShapeDtypeStruct((key_count, query_count), F32),
            out(own.shape[0], heads * nope_width), out(own.shape[0], heads * value_width),
        ],
        scratch_shapes=[
            pltpu.VMEM((query_count, heads, nope_width), BF16),
            pltpu.VMEM((query_count, heads, value_width), BF16),
            pltpu.VMEM((query_count * heads, nope_width), F32),
            pltpu.VMEM((1, query_count), jnp.int32),
            pltpu.SMEM((1, table.shape[1]), jnp.int32),
            pltpu.SemaphoreType.DMA((8,)),
        ],
        compiler_params=params(16),
        cost_estimate=cost(600_000_000, 12_000_000),
        name="prepare",
    )(*(pltpu.with_memory_space_constraint(x, pltpu.HBM) for x in (nope, rope, go, key_up, value_up, own, pos, table)))


def turned_values(paired, latent, vt_ref):
    slices, depth = vt_ref.shape[:2]
    turned = jnp.transpose(latent.astype(F32)).astype(BF16)
    for s in range(slices):
        vt_ref[place_of(paired, s)] = turned[s * depth:(s + 1) * depth]


def place_of(paired, s):
    if not paired:
        return s
    return jnp.bitwise_xor(s % 2, lax.axis_index("dp")) * 2 + jnp.bitwise_xor(s // 2, lax.axis_index("ctx"))


def weight_group(paired, at, qt, ds, gv, latent, vt_ref, bp_ref, outs):
    slices = vt_ref.shape[0]
    nope_slice = bp_ref.shape[1] // len(ds)
    value_width = gv.shape[1] // len(ds)
    for h in range(len(ds)):
        b = dot_nt(qt[h], ds[h]).astype(BF16)
        for s in range(slices):
            bp_ref[place_of(paired, s), h * nope_slice:(h + 1) * nope_slice] = b[s * nope_slice:(s + 1) * nope_slice]
    for s in range(slices):
        value_part = dot_nn(vt_ref[s], gv).astype(BF16)
        key_part = dot_nn(bp_ref[s], latent).astype(BF16)
        for h in range(len(ds)):
            rows = key_part[h * nope_slice:(h + 1) * nope_slice]
            columns = value_part[:, h * value_width:(h + 1) * value_width]
            if paired:
                for j in range(latent.shape[1] // value_width):
                    outs[s][at + h, 0, j * nope_slice:(j + 1) * nope_slice] = rows[:, j * value_width:(j + 1) * value_width]
                outs[s][at + h, 1] = columns
            else:
                outs[0][at + h] = rows
                outs[1][at + h] = columns


def attend_kernel(paired, first, final, weights, parts, begin, count, latent_width, qt_ref, go_ref, ku_ref, vu_ref, bias_ref, kn_own, va_own, *rest):
    rest = list(rest)
    part_refs = [rest.pop(0) for _ in range(parts)]
    before_ref = None if first else rest.pop(0)
    ds_ref, kn_ref = rest.pop(0), rest.pop(0)
    gv_ref = None if weights else rest.pop(0)
    outs = [rest.pop(0) for _ in range(4 if paired else 2)] if weights else None
    total_refs = [rest.pop(0) for _ in range(parts if final else 1)]
    nope_width = ku_ref.shape[1]
    value_width = vu_ref.shape[2]
    latent = jnp.concatenate([r[:, :latent_width] for r in part_refs], axis=0)
    rotary = jnp.concatenate([r[:, latent_width:] for r in part_refs], axis=0)
    if weights:
        vt_ref, bp_ref = rest
        turned_values(paired, latent, vt_ref)
        group = bp_ref.shape[1] * bp_ref.shape[0] // nope_width
    else:
        group = min(4, count)
    if not first:
        total = before_ref[...]
        total_latent, total_rotary = total[:, :latent_width], total[:, latent_width:]
    for g in range(0, count, group):
        at = begin + g
        heads = range(at, at + group)
        ku = ku_ref[at:at + group].reshape(group * nope_width, latent_width)
        vu = jnp.concatenate([vu_ref[h] for h in heads], axis=1)
        kn, values = kn_own[:, at * nope_width:(at + group) * nope_width], va_own[:, at * value_width:(at + group) * value_width]
        if parts == 2:
            far = latent[latent.shape[0] // 2:]
            kn = jnp.concatenate([kn, dot_nt(far, ku).astype(BF16)], axis=0)
            values = jnp.concatenate([values, dot_nn(far, vu).astype(BF16)], axis=0)
        raw = []
        for i, h in enumerate(heads):
            kn_h = kn[:, i * nope_width:(i + 1) * nope_width]
            kn_ref[g + i] = kn_h
            raw.append((
                dot_nn(jnp.concatenate([kn_h, rotary], axis=1), qt_ref[h]),
                dot_nt(values[:, i * value_width:(i + 1) * value_width], go_ref[h]),
            ))
        soft = []
        for scores, grad_probs in raw:
            scores = scores * softmax_scale + bias_ref[...]
            top = jnp.max(scores, axis=0, keepdims=True)
            weight = jnp.exp(scores - top)
            inverse = 1.0 / jnp.sum(weight, axis=0, keepdims=True)
            delta = jnp.sum(weight * grad_probs, axis=0, keepdims=True) * inverse
            probs = weight * inverse
            soft.append((probs.astype(BF16), (probs * ((grad_probs - delta) * softmax_scale)).astype(BF16)))
        gkn, gv = [], []
        rotary_sum = None
        for i, h in enumerate(heads):
            probs, ds = soft[i]
            ds_ref[g + i] = ds
            gk = dot_nt(ds, qt_ref[h])
            gkn.append(gk[:, :nope_width].astype(BF16))
            rotary_sum = gk[:, nope_width:] if rotary_sum is None else rotary_sum + gk[:, nope_width:]
            gv.append(dot_nn(probs, go_ref[h]).astype(BF16))
        gv = jnp.concatenate(gv, axis=1)
        latent_sum = dot_nn(jnp.concatenate(gkn, axis=1), ku) + dot_nt(gv, vu)
        if first and g == 0:
            total_latent, total_rotary = latent_sum, rotary_sum
        else:
            total_latent, total_rotary = total_latent + latent_sum, total_rotary + rotary_sum
        if weights:
            weight_group(paired, g, [qt_ref[h, :nope_width] for h in heads], [d for _, d in soft], gv, latent, vt_ref, bp_ref, outs)
        else:
            gv_ref[:, g * value_width:(g + group) * value_width] = gv
    start = 0
    for ref in total_refs:
        stop = start + ref.shape[0]
        ref[:, :latent_width] = total_latent[start:stop].astype(ref.dtype)
        ref[:, latent_width:] = total_rotary[start:stop].astype(ref.dtype)
        start = stop


def partial_shapes(paired, count, nope_width, latent_width, value_width):
    if paired:
        return [jax.ShapeDtypeStruct((count, 2, latent_width // 4, value_width), BF16)] * 4
    return [
        jax.ShapeDtypeStruct((count, nope_width, latent_width), BF16),
        jax.ShapeDtypeStruct((count, latent_width, value_width), BF16),
    ]


def partial_scratch(paired, group, key_count, nope_width, latent_width):
    slices = 4 if paired else 1
    return [
        pltpu.VMEM((slices, latent_width // slices, key_count), BF16),
        pltpu.VMEM((slices, group * nope_width // slices, key_count), BF16),
    ]


def attend(paired, begin, count, weights, final, qt, go, key_up, value_up, bias, kn_own, va_own, parts, before):
    _, nope_width, latent_width = key_up.shape
    value_width = value_up.shape[2]
    key_count, query_count = bias.shape
    row_width = parts[0].shape[1]
    out = lambda *dims: jax.ShapeDtypeStruct(dims, BF16)
    shapes = [out(count, key_count, query_count), out(count, key_count, nope_width)]
    if weights:
        shapes += partial_shapes(paired, count, nope_width, latent_width, value_width)
    else:
        shapes += [out(key_count, count * value_width)]
    shapes += [out(*p.shape) for p in parts] if final else [jax.ShapeDtypeStruct((key_count, row_width), F32)]
    group = min(4, count) if paired else 1
    return pl.pallas_call(
        functools.partial(attend_kernel, paired, before is None, final, weights, len(parts), begin, count, latent_width),
        out_shape=shapes,
        scratch_shapes=partial_scratch(paired, group, key_count, nope_width, latent_width) if weights else [],
        compiler_params=params(14 if paired else 56),
        cost_estimate=cost(count * (400_000_000 if weights else 300_000_000), count * 500_000),
        name="attend",
    )(qt, go, key_up, value_up, bias, kn_own, va_own, *parts, *([] if before is None else [before]))


def weights_kernel(paired, parts, begin, latent_width, qt_ref, ds_ref, gv_ref, *rest):
    part_refs, outs, vt_ref, bp_ref = rest[:parts], rest[parts:-2], rest[-2], rest[-1]
    latent = jnp.concatenate([r[:, :latent_width] for r in part_refs], axis=0)
    turned_values(paired, latent, vt_ref)
    count = ds_ref.shape[0]
    value_width = gv_ref.shape[1] // count
    nope_width = bp_ref.shape[1] if not paired else gv_ref.shape[1] // count
    group = min(4, count)
    for g in range(0, count, group):
        weight_group(
            paired, g, [qt_ref[begin + g + i, :nope_width] for i in range(group)], [ds_ref[g + i] for i in range(group)],
            gv_ref[:, g * value_width:(g + group) * value_width], latent, vt_ref, bp_ref, outs,
        )


def weight_partials(paired, begin, qt, ds, gv, parts, nope_width, latent_width):
    count, key_count, _ = ds.shape
    return pl.pallas_call(
        functools.partial(weights_kernel, paired, len(parts), begin, latent_width),
        out_shape=partial_shapes(paired, count, nope_width, latent_width, gv.shape[1] // count),
        scratch_shapes=partial_scratch(paired, min(4, count), key_count, nope_width, latent_width),
        compiler_params=params(14),
        cost_estimate=cost(count * 100_000_000, count * 400_000),
        name="weight_partials",
    )(qt, ds, gv, *parts)


def query_kernel(counts, parts, *refs):
    rotary_refs, refs = refs[:parts], refs[parts:]
    nope_ref, rope_ref = refs[-2:]
    rotary = jnp.concatenate([r[...] for r in rotary_refs], axis=0)
    nope_width = nope_ref.shape[1]
    rotary = rotary[:, rotary.shape[1] - rope_ref.shape[1]:]
    heads = sum(counts)
    query_count = rope_ref.shape[2]
    head = 0
    for c, count in enumerate(counts):
        ds_ref, kn_ref = refs[2 * c], refs[2 * c + 1]
        for h in range(count):
            ds = ds_ref[h]
            nope_ref[pl.ds(head, query_count, stride=heads), :] = dot_tn(ds, kn_ref[h])
            rope_ref[head] = dot_tn(rotary, ds)
            head += 1


def query_gradient(pairs, parts, rope_width):
    counts = [ds.shape[0] for ds, _ in pairs]
    heads = sum(counts)
    query_count, nope_width = pairs[0][0].shape[2], pairs[0][1].shape[2]
    nope, rope = pl.pallas_call(
        functools.partial(query_kernel, counts, len(parts)),
        out_shape=[
            jax.ShapeDtypeStruct((query_count * heads, nope_width), F32),
            jax.ShapeDtypeStruct((heads, rope_width, query_count), F32),
        ],
        compiler_params=params(8),
        cost_estimate=pl.CostEstimate(flops=1_000_000_000, bytes_accessed=5_000_000, transcendentals=0),
        name="query_gradient",
    )(*parts, *[x for pair in pairs for x in pair])
    return nope.reshape(1, query_count, heads, nope_width), jnp.transpose(rope, (2, 0, 1))[None]


def finish_kernel(own_ref, near_ref, far_ref, *rest):
    key_ref, value_ref = rest[-2:]
    rows = key_ref.shape[1]
    width = own_ref.shape[3]
    for h in range(key_ref.shape[0]):
        total = own_ref[h].astype(F32) + near_ref[h].astype(F32) + far_ref[h].astype(F32)
        for j in range(key_ref.shape[2] // width):
            key_ref[h, :, j * width:(j + 1) * width] = total[0, j * rows:(j + 1) * rows]
        value_ref[h] = total[1]


def finish(own, near, far, heads, begin, before, group):
    count, _, depth, width = own.shape
    rows = depth // 4
    offset = begin // group
    return pl.pallas_call(
        finish_kernel,
        grid=(count // group,),
        in_specs=[pl.BlockSpec((group, 2, depth, width), lambda i: (i, 0, 0, 0))] * 3
        + [pl.BlockSpec(memory_space=pl.ANY)] * len(before),
        out_specs=[
            pl.BlockSpec((group, rows, 4 * width), lambda i: (i + offset, 0, 0)),
            pl.BlockSpec((group, depth, width), lambda i: (i + offset, 0, 0)),
        ],
        out_shape=[
            jax.ShapeDtypeStruct((heads, rows, 4 * width), F32),
            jax.ShapeDtypeStruct((heads, depth, width), F32),
        ],
        input_output_aliases={3: 0, 4: 1} if before else {},
        compiler_params=params(8),
        cost_estimate=pl.CostEstimate(flops=1_000_000, bytes_accessed=300_000 * count, transcendentals=0),
        name="finish",
    )(own, near, far, *before)


def swap(x, axis, size, bits):
    return lax.ppermute(x, axis, [(i, i ^ bits) for i in range(size)])


def on_device(
    sizes, query_nope, query_rope, query_pos, latent_cache, block_table, key_up, value_up, grad_out
):
    head_size, ctx_size, dp_size = sizes
    heads, nope_width, latent_width = key_up.shape
    value_width = value_up.shape[2]
    page_rows, row_width = latent_cache.shape[2:]
    paired = (
        ctx_size == 2 and dp_size == 2 and latent_width == 4 * value_width and nope_width == value_width
        and nope_width % 64 == 0 and value_width % 128 == 0 and heads % 16 == 0
    )
    own_rows = latent_cache[0].reshape(-1, row_width)
    if ctx_size == 2:
        parts = [own_rows, swap(own_rows, "ctx", 2, 1)]
    else:
        parts = [lax.all_gather(own_rows, "ctx", axis=0, tiled=True)]
    rope = jnp.transpose(query_rope[0], (1, 2, 0))
    if paired:
        qt, go, ku, vu, own, bias, kn_own, va_own = prepare(
            2, query_nope[0], rope, grad_out[0], key_up, value_up, own_rows, query_pos, block_table, page_rows
        )
        parts[0] = own
        plan = [(heads * n // 16, weights) for n, weights in PLAN]
    else:
        qt = jnp.concatenate([jnp.transpose(query_nope[0], (1, 2, 0)), rope], axis=1)
        go, ku, vu = jnp.swapaxes(grad_out[0], 0, 1), key_up, value_up
        if ctx_size == 2:
            first = lax.axis_index("ctx") == 0
            parts = [jnp.concatenate([jnp.where(first, parts[0], parts[1]), jnp.where(first, parts[1], parts[0])], axis=0)]
        slots = jnp.arange(block_table.shape[1], dtype=jnp.int32)
        logical = jnp.sum(jnp.where(block_table[0][None, :] == slots[:, None], slots[None, :], 0), axis=1)
        positions = (logical[:, None] * page_rows + jnp.arange(page_rows, dtype=jnp.int32)[None, :]).reshape(-1, 1)
        bias = jnp.where(positions <= query_pos, 0.0, -jnp.inf).astype(F32)
        latent = parts[0][:, :latent_width]
        kn_own = jnp.einsum("kl,hnl->khn", latent, key_up, preferred_element_type=F32).astype(BF16).reshape(latent.shape[0], -1)
        va_own = jnp.einsum("kl,hlv->khv", latent, value_up, preferred_element_type=F32).astype(BF16).reshape(latent.shape[0], -1)
        plan = [(1, True)] * heads
    pairs, pieces, partials, total = [], [], [], None
    begin = 0
    for n, (count, weights) in enumerate(plan):
        final = n == len(plan) - 1
        results = list(attend(
            paired, begin, count, weights, final, qt, go, ku, vu, bias, kn_own, va_own, parts, total,
        ))
        pairs.append((results[0], results[1]))
        ends = results[-len(parts):] if final else results[-1:]
        if weights:
            made = results[2:len(results) - len(ends)]
        else:
            made = weight_partials(paired, begin, qt, results[0], results[2], parts, nope_width, latent_width)
        partials.append((begin, made))
        total = ends[0]
        begin += count
    if paired:
        for begin, (keep0, keep1, send0, send1) in partials:
            near1 = swap(send1, "dp", 2, 1)
            near0 = swap(send0, "dp", 2, 1)
            far = swap((keep1.astype(F32) + near1.astype(F32)).astype(BF16), "ctx", 2, 1)
            pieces.append((begin, (keep0, near0, far)))
        grad_nope, grad_rope = query_gradient(pairs, parts, query_rope.shape[3])
        mine, other = ends
        share = mine.astype(F32) + swap(other, "ctx", 2, 1).astype(F32)
    else:
        ds, kn = (jnp.concatenate(x, axis=0) for x in zip(*pairs))
        wk, wv = (jnp.concatenate(x, axis=0) for x in zip(*(made for _, made in partials)))
        grad_nope = jnp.einsum("hkq,hkn->qhn", ds, kn, preferred_element_type=F32)[None]
        rotary = parts[0][:, latent_width:]
        grad_rope = jnp.einsum("hkq,kr->qhr", ds, rotary, preferred_element_type=F32)[None]
        grad_key_map = lax.psum_scatter(wk, ("ctx", "dp"), scatter_dimension=1, tiled=True).astype(F32)
        grad_value_map = lax.psum_scatter(wv, ("ctx", "dp"), scatter_dimension=1, tiled=True).astype(F32)
        share = lax.psum_scatter(ends[0], "ctx", scatter_dimension=0, tiled=True).astype(F32)
    if head_size & (head_size - 1) == 0:
        bits = 1
        while bits < head_size:
            rounded = share.astype(BF16)
            got = swap(rounded, "head", head_size, bits | (bits >> 1) if bits >= 4 else bits)
            share = rounded.astype(F32) + got.astype(F32)
            bits *= 2
    else:
        share = lax.psum(share.astype(BF16), "head").astype(F32)
    if paired:
        maps = ()
        for begin, piece in pieces:
            maps = finish(*piece, heads, begin, maps, min(4, piece[0].shape[0]))
        grad_key_map, grad_value_map = maps
    return (
        grad_nope,
        grad_rope,
        share.reshape(latent_cache.shape),
        grad_key_map,
        grad_value_map,
    )


def solution(mesh):
    sizes = tuple(mesh.shape[axis] for axis in ("head", "ctx", "dp"))
    placed = (
        P("dp", "ctx", "head", None),
        P("dp", "ctx", "head", None),
        P("dp", "ctx"),
        P("dp", "ctx", None, None),
        P("dp", None),
        P("head", None, None),
        P("head", None, None),
        P("dp", "ctx", "head", None),
    )
    return jax.shard_map(
        functools.partial(on_device, sizes),
        mesh=mesh,
        in_specs=placed,
        out_specs=(
            P("dp", "ctx", "head", None),
            P("dp", "ctx", "head", None),
            P("dp", "ctx", None, None),
            P("head", ("ctx", "dp"), None),
            P("head", ("ctx", "dp"), None),
        ),
        check_vma=False,
    )
```

```python
import functools
import math

import jax
import jax.numpy as jnp
from jax import lax
from jax.experimental import pallas as pl
from jax.experimental.pallas import tpu as pltpu
from jax.sharding import PartitionSpec as P

softmax_scale = 192.0 ** (-0.5)
F32 = jnp.float32
BF16 = jnp.bfloat16
MIB = 1024 * 1024
PLAN = ((4, True, (4,)), (12, False, (12,)))
WAITS = (None, None)
FARS = {2: (0,)}
NEARS = {}
FRONT = True


def dot_nn(a, b):
    return lax.dot_general(a, b, (((1,), (0,)), ((), ())), preferred_element_type=F32)


def dot_nt(a, b):
    return lax.dot_general(a, b, (((1,), (1,)), ((), ())), preferred_element_type=F32)


def dot_tn(a, b):
    return lax.dot_general(a, b, (((0,), (0,)), ((), ())), preferred_element_type=F32)


def params(mib):
    return pltpu.CompilerParams(vmem_limit_bytes=mib * MIB)


def cost(flops, moved):
    return pl.CostEstimate(flops=flops, bytes_accessed=moved, transcendentals=0)


def prepare_kernel(
    parts, page_rows, nope_hbm, rope_hbm, go_hbm, ku_hbm, vu_hbm, own_hbm, pos_hbm, table_hbm,
    qt_ref, go_ref, ku_ref, vu_ref, own_ref, bias_ref, kn_ref, va_ref,
    nope_in, go_in, rows_ref, pos_ref, table_ref, sems,
):
    heads, nope_width, latent_width = ku_ref.shape
    value_width = vu_ref.shape[2]
    query_count = go_ref.shape[1]
    moves = (
        (nope_hbm, nope_in), (go_hbm, go_in), (own_hbm, own_ref), (ku_hbm, ku_ref), (vu_hbm, vu_ref),
        (rope_hbm, qt_ref.at[:, nope_width:, :]), (table_hbm, table_ref), (pos_hbm, pos_ref),
    )
    copies = [pltpu.make_async_copy(a, b, sems.at[i]) for i, (a, b) in enumerate(moves)]
    for copy in copies:
        copy.start()
    copies[0].wait()
    rows_ref[...] = nope_in[...].astype(F32).reshape(query_count * heads, nope_width)
    for h in range(heads):
        qt_ref[h, :nope_width] = jnp.transpose(rows_ref[pl.ds(h, query_count, stride=heads), :]).astype(BF16)
    copies[1].wait()
    rows_ref[...] = go_in[...].astype(F32).reshape(query_count * heads, nope_width)
    for h in range(heads):
        go_ref[h] = rows_ref[pl.ds(h, query_count, stride=heads), :].astype(BF16)
    copies[6].wait()
    copies[7].wait()
    blocks = table_ref.shape[1]
    row = lax.broadcasted_iota(jnp.int32, (page_rows, query_count), 0)
    part_blocks = blocks // parts
    for i in range(blocks):
        slot = jnp.bitwise_xor(lax.axis_index("ctx"), i // part_blocks) * part_blocks + i % part_blocks if parts == 2 else i
        logical = jnp.int32(0)
        for b in range(blocks):
            logical = logical + jnp.where(table_ref[0, b] == slot, b, 0)
        visible = row + logical * page_rows <= pos_ref[...]
        bias_ref[i * page_rows:(i + 1) * page_rows] = jnp.where(visible, 0.0, -jnp.inf)
    copies[2].wait()
    latent = own_ref[:, :latent_width]
    copies[3].wait()
    step = 2
    for h in range(0, heads, step):
        ku = ku_ref[h:h + step].reshape(step * nope_width, latent_width)
        kn_ref[:, h * nope_width:(h + step) * nope_width] = dot_nt(latent, ku).astype(BF16)
    copies[4].wait()
    for h in range(0, heads, step):
        vu = jnp.concatenate([vu_ref[h + i] for i in range(step)], axis=1)
        va_ref[:, h * value_width:(h + step) * value_width] = dot_nn(latent, vu).astype(BF16)
    copies[5].wait()


def prepare(parts, nope, rope, go, key_up, value_up, own, pos, table, page_rows):
    query_count, heads, nope_width = nope.shape
    value_width = go.shape[2]
    key_count = table.shape[1] * page_rows
    out = lambda *dims: jax.ShapeDtypeStruct(dims, BF16)
    hbm = pl.BlockSpec(memory_space=pltpu.HBM)
    return pl.pallas_call(
        functools.partial(prepare_kernel, parts, page_rows),
        in_specs=[hbm] * 8,
        out_specs=[pl.BlockSpec(memory_space=pltpu.VMEM)] * 8,
        out_shape=[
            out(heads, nope_width + rope.shape[1], query_count), out(heads, query_count, value_width),
            out(*key_up.shape), out(*value_up.shape), out(*own.shape),
            jax.ShapeDtypeStruct((key_count, query_count), F32),
            out(own.shape[0], heads * nope_width), out(own.shape[0], heads * value_width),
        ],
        scratch_shapes=[
            pltpu.VMEM((query_count, heads, nope_width), BF16),
            pltpu.VMEM((query_count, heads, value_width), BF16),
            pltpu.VMEM((query_count * heads, nope_width), F32),
            pltpu.VMEM((1, query_count), jnp.int32),
            pltpu.SMEM((1, table.shape[1]), jnp.int32),
            pltpu.SemaphoreType.DMA((8,)),
        ],
        compiler_params=params(16),
        cost_estimate=cost(600_000_000, 12_000_000),
        name="prepare",
    )(*(pltpu.with_memory_space_constraint(x, pltpu.HBM) for x in (nope, rope, go, key_up, value_up, own, pos, table)))


def turned_values(paired, latent, vt_ref):
    slices, depth = vt_ref.shape[:2]
    turned = jnp.transpose(latent.astype(F32)).astype(BF16)
    for s in range(slices):
        vt_ref[place_of(paired, s)] = turned[s * depth:(s + 1) * depth]


def place_of(paired, s):
    if not paired:
        return s
    return jnp.bitwise_xor(s % 2, lax.axis_index("dp")) * 2 + jnp.bitwise_xor(s // 2, lax.axis_index("ctx"))


def weight_group(paired, at, qt, ds, gv, latent, vt_ref, bp_ref, outs):
    slices = vt_ref.shape[0]
    nope_slice = bp_ref.shape[1] // len(ds)
    value_width = gv.shape[1] // len(ds)
    for h in range(len(ds)):
        b = dot_nt(qt[h], ds[h]).astype(BF16)
        for s in range(slices):
            bp_ref[place_of(paired, s), h * nope_slice:(h + 1) * nope_slice] = b[s * nope_slice:(s + 1) * nope_slice]
    for s in range(slices):
        value_part = dot_nn(vt_ref[s], gv).astype(BF16)
        key_part = dot_nn(bp_ref[s], latent).astype(BF16)
        for h in range(len(ds)):
            rows = key_part[h * nope_slice:(h + 1) * nope_slice]
            columns = value_part[:, h * value_width:(h + 1) * value_width]
            if paired:
                for j in range(latent.shape[1] // value_width):
                    outs[s][at + h, 0, j * nope_slice:(j + 1) * nope_slice] = rows[:, j * value_width:(j + 1) * value_width]
                outs[s][at + h, 1] = columns
            else:
                outs[0][at + h] = rows
                outs[1][at + h] = columns


def attend_kernel(paired, first, final, weights, parts, begin, count, latent_width, qt_ref, go_ref, ku_ref, vu_ref, bias_ref, kn_own, va_own, *rest):
    rest = list(rest)
    part_refs = [rest.pop(0) for _ in range(parts)]
    before_ref = None if first else rest.pop(0)
    ds_ref, kn_ref = rest.pop(0), rest.pop(0)
    gv_ref = None if weights else rest.pop(0)
    outs = [rest.pop(0) for _ in range(4 if paired else 2)] if weights else None
    total_refs = [rest.pop(0) for _ in range(parts if final else 1)]
    nope_width = ku_ref.shape[1]
    value_width = vu_ref.shape[2]
    latent = jnp.concatenate([r[:, :latent_width] for r in part_refs], axis=0)
    rotary = jnp.concatenate([r[:, latent_width:] for r in part_refs], axis=0)
    if weights:
        vt_ref, bp_ref = rest
        turned_values(paired, latent, vt_ref)
        group = bp_ref.shape[1] * bp_ref.shape[0] // nope_width
    else:
        group = min(4, count)
    if not first:
        total = before_ref[...]
        total_latent, total_rotary = total[:, :latent_width], total[:, latent_width:]
    for g in range(0, count, group):
        at = begin + g
        heads = range(at, at + group)
        ku = ku_ref[at:at + group].reshape(group * nope_width, latent_width)
        vu = jnp.concatenate([vu_ref[h] for h in heads], axis=1)
        kn, values = kn_own[:, at * nope_width:(at + group) * nope_width], va_own[:, at * value_width:(at + group) * value_width]
        if parts == 2:
            far = latent[latent.shape[0] // 2:]
            kn = jnp.concatenate([kn, dot_nt(far, ku).astype(BF16)], axis=0)
            values = jnp.concatenate([values, dot_nn(far, vu).astype(BF16)], axis=0)
        raw = []
        for i, h in enumerate(heads):
            kn_h = kn[:, i * nope_width:(i + 1) * nope_width]
            kn_ref[g + i] = kn_h
            raw.append((
                dot_nn(jnp.concatenate([kn_h, rotary], axis=1), qt_ref[h]),
                dot_nt(values[:, i * value_width:(i + 1) * value_width], go_ref[h]),
            ))
        soft = []
        for scores, grad_probs in raw:
            scores = scores * softmax_scale + bias_ref[...]
            top = jnp.max(scores, axis=0, keepdims=True)
            weight = jnp.exp(scores - top)
            inverse = 1.0 / jnp.sum(weight, axis=0, keepdims=True)
            delta = jnp.sum(weight * grad_probs, axis=0, keepdims=True) * inverse
            probs = weight * inverse
            soft.append((probs.astype(BF16), (probs * ((grad_probs - delta) * softmax_scale)).astype(BF16)))
        gkn, gv = [], []
        rotary_sum = None
        for i, h in enumerate(heads):
            probs, ds = soft[i]
            ds_ref[g + i] = ds
            gk = dot_nt(ds, qt_ref[h])
            gkn.append(gk[:, :nope_width].astype(BF16))
            rotary_sum = gk[:, nope_width:] if rotary_sum is None else rotary_sum + gk[:, nope_width:]
            gv.append(dot_nn(probs, go_ref[h]).astype(BF16))
        gv = jnp.concatenate(gv, axis=1)
        latent_sum = dot_nn(jnp.concatenate(gkn, axis=1), ku) + dot_nt(gv, vu)
        if first and g == 0:
            total_latent, total_rotary = latent_sum, rotary_sum
        else:
            total_latent, total_rotary = total_latent + latent_sum, total_rotary + rotary_sum
        if weights:
            weight_group(paired, g, [qt_ref[h, :nope_width] for h in heads], [d for _, d in soft], gv, latent, vt_ref, bp_ref, outs)
        else:
            gv_ref[:, g * value_width:(g + group) * value_width] = gv
    start = 0
    for ref in total_refs:
        stop = start + ref.shape[0]
        ref[:, :latent_width] = total_latent[start:stop].astype(ref.dtype)
        ref[:, latent_width:] = total_rotary[start:stop].astype(ref.dtype)
        start = stop


def partial_shapes(paired, count, nope_width, latent_width, value_width):
    if paired:
        return [jax.ShapeDtypeStruct((count, 2, latent_width // 4, value_width), BF16)] * 4
    return [
        jax.ShapeDtypeStruct((count, nope_width, latent_width), BF16),
        jax.ShapeDtypeStruct((count, latent_width, value_width), BF16),
    ]


def partial_scratch(paired, group, key_count, nope_width, latent_width):
    slices = 4 if paired else 1
    return [
        pltpu.VMEM((slices, latent_width // slices, key_count), BF16),
        pltpu.VMEM((slices, group * nope_width // slices, key_count), BF16),
    ]


def attend(paired, begin, count, weights, final, qt, go, key_up, value_up, bias, kn_own, va_own, parts, before):
    _, nope_width, latent_width = key_up.shape
    value_width = value_up.shape[2]
    key_count, query_count = bias.shape
    row_width = parts[0].shape[1]
    out = lambda *dims: jax.ShapeDtypeStruct(dims, BF16)
    shapes = [out(count, key_count, query_count), out(count, key_count, nope_width)]
    if weights:
        shapes += partial_shapes(paired, count, nope_width, latent_width, value_width)
    else:
        shapes += [out(key_count, count * value_width)]
    shapes += [out(*p.shape) for p in parts] if final else [jax.ShapeDtypeStruct((key_count, row_width), F32)]
    group = min(4, count) if paired else 1
    return pl.pallas_call(
        functools.partial(attend_kernel, paired, before is None, final, weights, len(parts), begin, count, latent_width),
        out_shape=shapes,
        scratch_shapes=partial_scratch(paired, group, key_count, nope_width, latent_width) if weights else [],
        compiler_params=params(14 if paired else 56),
        cost_estimate=cost(count * (400_000_000 if weights else 300_000_000), count * 500_000),
        name="attend",
    )(qt, go, key_up, value_up, bias, kn_own, va_own, *parts, *([] if before is None else [before]))


def weights_kernel(paired, parts, begin, latent_width, qt_ref, ds_ref, gv_ref, *rest):
    part_refs, outs, vt_ref, bp_ref = rest[:parts], rest[parts:-2], rest[-2], rest[-1]
    latent = jnp.concatenate([r[:, :latent_width] for r in part_refs], axis=0)
    turned_values(paired, latent, vt_ref)
    count = ds_ref.shape[0]
    value_width = gv_ref.shape[1] // count
    nope_width = bp_ref.shape[1] if not paired else gv_ref.shape[1] // count
    group = min(4, count)
    for g in range(0, count, group):
        weight_group(
            paired, g, [qt_ref[begin + g + i, :nope_width] for i in range(group)], [ds_ref[g + i] for i in range(group)],
            gv_ref[:, g * value_width:(g + group) * value_width], latent, vt_ref, bp_ref, outs,
        )


def weight_partials(paired, begin, qt, ds, gv, parts, nope_width, latent_width):
    count, key_count, _ = ds.shape
    return pl.pallas_call(
        functools.partial(weights_kernel, paired, len(parts), begin, latent_width),
        out_shape=partial_shapes(paired, count, nope_width, latent_width, gv.shape[1] // count),
        scratch_shapes=partial_scratch(paired, min(4, count), key_count, nope_width, latent_width),
        compiler_params=params(14),
        cost_estimate=cost(count * 100_000_000, count * 400_000),
        name="weight_partials",
    )(qt, ds, gv, *parts)


def query_kernel(counts, parts, *refs):
    rotary_refs, refs = refs[:parts], refs[parts:]
    nope_ref, rope_ref = refs[-2:]
    rotary = jnp.concatenate([r[...] for r in rotary_refs], axis=0)
    nope_width = nope_ref.shape[1]
    rotary = rotary[:, rotary.shape[1] - rope_ref.shape[1]:]
    heads = sum(counts)
    query_count = rope_ref.shape[2]
    head = 0
    for c, count in enumerate(counts):
        ds_ref, kn_ref = refs[2 * c], refs[2 * c + 1]
        for h in range(count):
            ds = ds_ref[h]
            nope_ref[pl.ds(head, query_count, stride=heads), :] = dot_tn(ds, kn_ref[h])
            rope_ref[head] = dot_tn(rotary, ds)
            head += 1


def query_gradient(pairs, parts, rope_width):
    counts = [ds.shape[0] for ds, _ in pairs]
    heads = sum(counts)
    query_count, nope_width = pairs[0][0].shape[2], pairs[0][1].shape[2]
    nope, rope = pl.pallas_call(
        functools.partial(query_kernel, counts, len(parts)),
        out_shape=[
            jax.ShapeDtypeStruct((query_count * heads, nope_width), F32),
            jax.ShapeDtypeStruct((heads, rope_width, query_count), F32),
        ],
        compiler_params=params(8),
        cost_estimate=pl.CostEstimate(flops=1_000_000_000, bytes_accessed=5_000_000, transcendentals=0),
        name="query_gradient",
    )(*parts, *[x for pair in pairs for x in pair])
    return nope.reshape(1, query_count, heads, nope_width), jnp.transpose(rope, (2, 0, 1))[None]


def finish_kernel(own_ref, near_ref, far_ref, *rest):
    key_ref, value_ref = rest[-2:]
    rows = key_ref.shape[1]
    width = own_ref.shape[3]
    for h in range(key_ref.shape[0]):
        total = own_ref[h].astype(F32) + near_ref[h].astype(F32) + far_ref[h].astype(F32)
        for j in range(key_ref.shape[2] // width):
            key_ref[h, :, j * width:(j + 1) * width] = total[0, j * rows:(j + 1) * rows]
        value_ref[h] = total[1]


def finish(own, near, far, inner, heads, begin, before, group):
    count, _, depth, width = far.shape
    rows = depth // 4
    inside, offset = inner // group, begin // group
    return pl.pallas_call(
        finish_kernel,
        grid=(count // group,),
        in_specs=[pl.BlockSpec((group, 2, depth, width), lambda i: (i + inside, 0, 0, 0))] * 2
        + [pl.BlockSpec((group, 2, depth, width), lambda i: (i, 0, 0, 0))]
        + [pl.BlockSpec(memory_space=pl.ANY)] * len(before),
        out_specs=[
            pl.BlockSpec((group, rows, 4 * width), lambda i: (i + offset, 0, 0)),
            pl.BlockSpec((group, depth, width), lambda i: (i + offset, 0, 0)),
        ],
        out_shape=[
            jax.ShapeDtypeStruct((heads, rows, 4 * width), F32),
            jax.ShapeDtypeStruct((heads, depth, width), F32),
        ],
        input_output_aliases={3: 0, 4: 1} if before else {},
        compiler_params=params(8),
        cost_estimate=pl.CostEstimate(flops=1_000_000, bytes_accessed=300_000 * count, transcendentals=0),
        name="finish",
    )(own, near, far, *before)


def swap(x, axis, size, bits):
    return lax.ppermute(x, axis, [(i, i ^ bits) for i in range(size)])


def after(x, arrays, which):
    for n in which:
        x, arrays[n] = lax.optimization_barrier((x, arrays[n]))
    return x


def on_device(
    sizes, query_nope, query_rope, query_pos, latent_cache, block_table, key_up, value_up, grad_out
):
    head_size, ctx_size, dp_size = sizes
    heads, nope_width, latent_width = key_up.shape
    value_width = value_up.shape[2]
    page_rows, row_width = latent_cache.shape[2:]
    paired = (
        ctx_size == 2 and dp_size == 2 and latent_width == 4 * value_width and nope_width == value_width
        and nope_width % 64 == 0 and value_width % 128 == 0 and heads % 16 == 0
    )
    own_rows = latent_cache[0].reshape(-1, row_width)
    if ctx_size == 2:
        parts = [own_rows, swap(own_rows, "ctx", 2, 1)]
    else:
        parts = [lax.all_gather(own_rows, "ctx", axis=0, tiled=True)]
    rope = jnp.transpose(query_rope[0], (1, 2, 0))
    if paired:
        qt, go, ku, vu, own, bias, kn_own, va_own = prepare(
            2, query_nope[0], rope, grad_out[0], key_up, value_up, own_rows, query_pos, block_table, page_rows
        )
        parts[0] = own
        plan = [(heads * n // 16, weights, [heads * c // 16 for c in cuts]) for n, weights, cuts in PLAN]
    else:
        qt = jnp.concatenate([jnp.transpose(query_nope[0], (1, 2, 0)), rope], axis=1)
        go, ku, vu = jnp.swapaxes(grad_out[0], 0, 1), key_up, value_up
        if ctx_size == 2:
            first = lax.axis_index("ctx") == 0
            parts = [jnp.concatenate([jnp.where(first, parts[0], parts[1]), jnp.where(first, parts[1], parts[0])], axis=0)]
        slots = jnp.arange(block_table.shape[1], dtype=jnp.int32)
        logical = jnp.sum(jnp.where(block_table[0][None, :] == slots[:, None], slots[None, :], 0), axis=1)
        positions = (logical[:, None] * page_rows + jnp.arange(page_rows, dtype=jnp.int32)[None, :]).reshape(-1, 1)
        bias = jnp.where(positions <= query_pos, 0.0, -jnp.inf).astype(F32)
        latent = parts[0][:, :latent_width]
        kn_own = jnp.einsum("kl,hnl->khn", latent, key_up, preferred_element_type=F32).astype(BF16).reshape(latent.shape[0], -1)
        va_own = jnp.einsum("kl,hlv->khv", latent, value_up, preferred_element_type=F32).astype(BF16).reshape(latent.shape[0], -1)
        plan = [(1, True, ())] * heads
    pairs, partials, pieces, fars, nears, total = [], [], [], [], [], None
    begin = 0
    for n, (count, weights, cuts) in enumerate(plan):
        final = n == len(plan) - 1
        results = list(attend(
            paired, begin, count, weights, final, qt, go, ku, vu, bias, kn_own, va_own, parts, total,
        ))
        pairs.append((results[0], results[1]))
        ends = results[-len(parts):] if final else results[-1:]
        if weights:
            made = results[2:len(results) - len(ends)]
        else:
            made = weight_partials(paired, begin, qt, results[0], results[2], parts, nope_width, latent_width)
        partials.append(made)
        total = ends[0]
        if paired:
            keep0, keep1, send0, send1 = made
            near1 = swap(send1, "dp", 2, 1)
            inner = 0
            for size in cuts:
                cut = slice(inner, inner + size)
                sent = (keep1[cut].astype(F32) + near1[cut].astype(F32)).astype(BF16)
                pieces.append((keep0, n, inner, begin + inner))
                if FRONT and n == len(plan) - 2:
                    total, sent = lax.optimization_barrier((total, sent))
                fars.append(swap(sent, "ctx", 2, 1))
                inner += size
            if WAITS[n] is not None:
                send0, fars[WAITS[n]] = lax.optimization_barrier((send0, fars[WAITS[n]]))
            nears.append(swap(send0, "dp", 2, 1))
        begin += count
    if paired:
        grad_nope, grad_rope = query_gradient(pairs, parts, query_rope.shape[3])
        mine, other = ends
        other = after(other, fars, FARS.get(0, ()))
        share = mine.astype(F32) + swap(other, "ctx", 2, 1).astype(F32)
    else:
        ds, kn = (jnp.concatenate(x, axis=0) for x in zip(*pairs))
        wk, wv = (jnp.concatenate(x, axis=0) for x in zip(*partials))
        grad_nope = jnp.einsum("hkq,hkn->qhn", ds, kn, preferred_element_type=F32)[None]
        rotary = parts[0][:, latent_width:]
        grad_rope = jnp.einsum("hkq,kr->qhr", ds, rotary, preferred_element_type=F32)[None]
        grad_key_map = lax.psum_scatter(wk, ("ctx", "dp"), scatter_dimension=1, tiled=True).astype(F32)
        grad_value_map = lax.psum_scatter(wv, ("ctx", "dp"), scatter_dimension=1, tiled=True).astype(F32)
        share = lax.psum_scatter(ends[0], "ctx", scatter_dimension=0, tiled=True).astype(F32)
    if head_size & (head_size - 1) == 0:
        bits, n = 1, 0
        while bits < head_size:
            rounded = share.astype(BF16)
            if paired:
                rounded = after(rounded, fars, FARS.get(n + 1, ()))
                rounded = after(rounded, nears, NEARS.get(n + 1, ()))
            got = swap(rounded, "head", head_size, bits | (bits >> 1) if bits >= 4 else bits)
            share = rounded.astype(F32) + got.astype(F32)
            bits, n = bits * 2, n + 1
    else:
        share = lax.psum(share.astype(BF16), "head").astype(F32)
    if paired:
        maps = ()
        for (own0, n, inner, begin), far in zip(pieces, fars):
            maps = finish(own0, nears[n], far, inner, heads, begin, maps, math.gcd(begin, inner, far.shape[0]))
        grad_key_map, grad_value_map = maps
    return (
        grad_nope,
        grad_rope,
        share.reshape(latent_cache.shape),
        grad_key_map,
        grad_value_map,
    )


def solution(mesh):
    sizes = tuple(mesh.shape[axis] for axis in ("head", "ctx", "dp"))
    placed = (
        P("dp", "ctx", "head", None),
        P("dp", "ctx", "head", None),
        P("dp", "ctx"),
        P("dp", "ctx", None, None),
        P("dp", None),
        P("head", None, None),
        P("head", None, None),
        P("dp", "ctx", "head", None),
    )
    return jax.shard_map(
        functools.partial(on_device, sizes),
        mesh=mesh,
        in_specs=placed,
        out_specs=(
            P("dp", "ctx", "head", None),
            P("dp", "ctx", "head", None),
            P("dp", "ctx", None, None),
            P("head", ("ctx", "dp"), None),
            P("head", ("ctx", "dp"), None),
        ),
        check_vma=False,
    )
```

```python
import functools
import math

import jax
import jax.numpy as jnp
from jax import lax
from jax.experimental import pallas as pl
from jax.experimental.pallas import tpu as pltpu
from jax.sharding import PartitionSpec as P

softmax_scale = 192.0 ** (-0.5)
F32 = jnp.float32
BF16 = jnp.bfloat16
MIB = 1024 * 1024
PLAN = ((4, True), (4, False), (4, False), (4, False))
CUTS = ((4,), (4,), (4,), (4,))
GROUPS = ((0,), (1,), (2,))
WAITS = (None, None, None, None)
FARS = {2: (0,)}
NEARS = {}
FRONT = 1
WEIGHT_COST = 100_000_000
JOIN = (2, 3)
LATE = True


def dot_nn(a, b):
    return lax.dot_general(a, b, (((1,), (0,)), ((), ())), preferred_element_type=F32)


def dot_nt(a, b):
    return lax.dot_general(a, b, (((1,), (1,)), ((), ())), preferred_element_type=F32)


def dot_tn(a, b):
    return lax.dot_general(a, b, (((0,), (0,)), ((), ())), preferred_element_type=F32)


def params(mib):
    return pltpu.CompilerParams(vmem_limit_bytes=mib * MIB)


def cost(flops, moved):
    return pl.CostEstimate(flops=flops, bytes_accessed=moved, transcendentals=0)


def prepare_kernel(
    parts, page_rows, nope_hbm, rope_hbm, go_hbm, ku_hbm, vu_hbm, own_hbm, pos_hbm, table_hbm,
    qt_ref, go_ref, ku_ref, vu_ref, own_ref, bias_ref, kn_ref, va_ref,
    nope_in, go_in, rows_ref, pos_ref, table_ref, sems,
):
    heads, nope_width, latent_width = ku_ref.shape
    value_width = vu_ref.shape[2]
    query_count = go_ref.shape[1]
    moves = (
        (nope_hbm, nope_in), (go_hbm, go_in), (own_hbm, own_ref), (ku_hbm, ku_ref), (vu_hbm, vu_ref),
        (rope_hbm, qt_ref.at[:, nope_width:, :]), (table_hbm, table_ref), (pos_hbm, pos_ref),
    )
    copies = [pltpu.make_async_copy(a, b, sems.at[i]) for i, (a, b) in enumerate(moves)]
    for copy in copies:
        copy.start()
    copies[0].wait()
    rows_ref[...] = nope_in[...].astype(F32).reshape(query_count * heads, nope_width)
    for h in range(heads):
        qt_ref[h, :nope_width] = jnp.transpose(rows_ref[pl.ds(h, query_count, stride=heads), :]).astype(BF16)
    copies[1].wait()
    rows_ref[...] = go_in[...].astype(F32).reshape(query_count * heads, nope_width)
    for h in range(heads):
        go_ref[h] = rows_ref[pl.ds(h, query_count, stride=heads), :].astype(BF16)
    copies[6].wait()
    copies[7].wait()
    blocks = table_ref.shape[1]
    row = lax.broadcasted_iota(jnp.int32, (page_rows, query_count), 0)
    part_blocks = blocks // parts
    for i in range(blocks):
        slot = jnp.bitwise_xor(lax.axis_index("ctx"), i // part_blocks) * part_blocks + i % part_blocks if parts == 2 else i
        logical = jnp.int32(0)
        for b in range(blocks):
            logical = logical + jnp.where(table_ref[0, b] == slot, b, 0)
        visible = row + logical * page_rows <= pos_ref[...]
        bias_ref[i * page_rows:(i + 1) * page_rows] = jnp.where(visible, 0.0, -jnp.inf)
    copies[2].wait()
    latent = own_ref[:, :latent_width]
    copies[3].wait()
    step = 2
    for h in range(0, heads, step):
        ku = ku_ref[h:h + step].reshape(step * nope_width, latent_width)
        kn_ref[:, h * nope_width:(h + step) * nope_width] = dot_nt(latent, ku).astype(BF16)
    copies[4].wait()
    for h in range(0, heads, step):
        vu = jnp.concatenate([vu_ref[h + i] for i in range(step)], axis=1)
        va_ref[:, h * value_width:(h + step) * value_width] = dot_nn(latent, vu).astype(BF16)
    copies[5].wait()


def prepare(parts, nope, rope, go, key_up, value_up, own, pos, table, page_rows):
    query_count, heads, nope_width = nope.shape
    value_width = go.shape[2]
    key_count = table.shape[1] * page_rows
    out = lambda *dims: jax.ShapeDtypeStruct(dims, BF16)
    hbm = pl.BlockSpec(memory_space=pltpu.HBM)
    return pl.pallas_call(
        functools.partial(prepare_kernel, parts, page_rows),
        in_specs=[hbm] * 8,
        out_specs=[pl.BlockSpec(memory_space=pltpu.VMEM)] * 8,
        out_shape=[
            out(heads, nope_width + rope.shape[1], query_count), out(heads, query_count, value_width),
            out(*key_up.shape), out(*value_up.shape), out(*own.shape),
            jax.ShapeDtypeStruct((key_count, query_count), F32),
            out(own.shape[0], heads * nope_width), out(own.shape[0], heads * value_width),
        ],
        scratch_shapes=[
            pltpu.VMEM((query_count, heads, nope_width), BF16),
            pltpu.VMEM((query_count, heads, value_width), BF16),
            pltpu.VMEM((query_count * heads, nope_width), F32),
            pltpu.VMEM((1, query_count), jnp.int32),
            pltpu.SMEM((1, table.shape[1]), jnp.int32),
            pltpu.SemaphoreType.DMA((8,)),
        ],
        compiler_params=params(16),
        cost_estimate=cost(600_000_000, 12_000_000),
        name="prepare",
    )(*(pltpu.with_memory_space_constraint(x, pltpu.HBM) for x in (nope, rope, go, key_up, value_up, own, pos, table)))


def turned_values(paired, latent, vt_ref):
    slices, depth = vt_ref.shape[:2]
    turned = jnp.transpose(latent.astype(F32)).astype(BF16)
    for s in range(slices):
        vt_ref[place_of(paired, s)] = turned[s * depth:(s + 1) * depth]


def place_of(paired, s):
    if not paired:
        return s
    return jnp.bitwise_xor(s % 2, lax.axis_index("dp")) * 2 + jnp.bitwise_xor(s // 2, lax.axis_index("ctx"))


def weight_group(paired, at, qt, ds, gv, latent, vt_ref, bp_ref, outs):
    slices = vt_ref.shape[0]
    nope_slice = bp_ref.shape[1] // len(ds)
    value_width = gv.shape[1] // len(ds)
    for h in range(len(ds)):
        b = dot_nt(qt[h], ds[h]).astype(BF16)
        for s in range(slices):
            bp_ref[place_of(paired, s), h * nope_slice:(h + 1) * nope_slice] = b[s * nope_slice:(s + 1) * nope_slice]
    for s in range(slices):
        value_part = dot_nn(vt_ref[s], gv).astype(BF16)
        key_part = dot_nn(bp_ref[s], latent).astype(BF16)
        for h in range(len(ds)):
            rows = key_part[h * nope_slice:(h + 1) * nope_slice]
            columns = value_part[:, h * value_width:(h + 1) * value_width]
            if paired:
                for j in range(latent.shape[1] // value_width):
                    outs[s][at + h, 0, j * nope_slice:(j + 1) * nope_slice] = rows[:, j * value_width:(j + 1) * value_width]
                outs[s][at + h, 1] = columns
            else:
                outs[0][at + h] = rows
                outs[1][at + h] = columns


def attend_kernel(paired, first, final, weights, parts, begin, count, latent_width, qt_ref, go_ref, ku_ref, vu_ref, bias_ref, kn_own, va_own, *rest):
    rest = list(rest)
    part_refs = [rest.pop(0) for _ in range(parts)]
    before_ref = None if first else rest.pop(0)
    ds_ref, kn_ref = rest.pop(0), rest.pop(0)
    gv_ref = None if weights else rest.pop(0)
    outs = [rest.pop(0) for _ in range(4 if paired else 2)] if weights else None
    total_refs = [rest.pop(0) for _ in range(parts if final else 1)]
    nope_width = ku_ref.shape[1]
    value_width = vu_ref.shape[2]
    latent = jnp.concatenate([r[:, :latent_width] for r in part_refs], axis=0)
    rotary = jnp.concatenate([r[:, latent_width:] for r in part_refs], axis=0)
    if weights:
        vt_ref, bp_ref = rest
        turned_values(paired, latent, vt_ref)
        group = bp_ref.shape[1] * bp_ref.shape[0] // nope_width
    else:
        group = min(4, count)
    if not first:
        total = before_ref[...]
        total_latent, total_rotary = total[:, :latent_width], total[:, latent_width:]
    for g in range(0, count, group):
        at = begin + g
        heads = range(at, at + group)
        ku = ku_ref[at:at + group].reshape(group * nope_width, latent_width)
        vu = jnp.concatenate([vu_ref[h] for h in heads], axis=1)
        kn, values = kn_own[:, at * nope_width:(at + group) * nope_width], va_own[:, at * value_width:(at + group) * value_width]
        if parts == 2:
            far = latent[latent.shape[0] // 2:]
            kn = jnp.concatenate([kn, dot_nt(far, ku).astype(BF16)], axis=0)
            values = jnp.concatenate([values, dot_nn(far, vu).astype(BF16)], axis=0)
        raw = []
        for i, h in enumerate(heads):
            kn_h = kn[:, i * nope_width:(i + 1) * nope_width]
            kn_ref[g + i] = kn_h
            raw.append((
                dot_nn(jnp.concatenate([kn_h, rotary], axis=1), qt_ref[h]),
                dot_nt(values[:, i * value_width:(i + 1) * value_width], go_ref[h]),
            ))
        soft = []
        for scores, grad_probs in raw:
            scores = scores * softmax_scale + bias_ref[...]
            top = jnp.max(scores, axis=0, keepdims=True)
            weight = jnp.exp(scores - top)
            inverse = 1.0 / jnp.sum(weight, axis=0, keepdims=True)
            delta = jnp.sum(weight * grad_probs, axis=0, keepdims=True) * inverse
            probs = weight * inverse
            soft.append((probs.astype(BF16), (probs * ((grad_probs - delta) * softmax_scale)).astype(BF16)))
        gkn, gv = [], []
        rotary_sum = None
        for i, h in enumerate(heads):
            probs, ds = soft[i]
            ds_ref[g + i] = ds
            gk = dot_nt(ds, qt_ref[h])
            gkn.append(gk[:, :nope_width].astype(BF16))
            rotary_sum = gk[:, nope_width:] if rotary_sum is None else rotary_sum + gk[:, nope_width:]
            gv.append(dot_nn(probs, go_ref[h]).astype(BF16))
        gv = jnp.concatenate(gv, axis=1)
        latent_sum = dot_nn(jnp.concatenate(gkn, axis=1), ku) + dot_nt(gv, vu)
        if first and g == 0:
            total_latent, total_rotary = latent_sum, rotary_sum
        else:
            total_latent, total_rotary = total_latent + latent_sum, total_rotary + rotary_sum
        if weights:
            weight_group(paired, g, [qt_ref[h, :nope_width] for h in heads], [d for _, d in soft], gv, latent, vt_ref, bp_ref, outs)
        else:
            gv_ref[:, g * value_width:(g + group) * value_width] = gv
    start = 0
    for ref in total_refs:
        stop = start + ref.shape[0]
        ref[:, :latent_width] = total_latent[start:stop].astype(ref.dtype)
        ref[:, latent_width:] = total_rotary[start:stop].astype(ref.dtype)
        start = stop


def partial_shapes(paired, count, nope_width, latent_width, value_width):
    if paired:
        return [jax.ShapeDtypeStruct((count, 2, latent_width // 4, value_width), BF16)] * 4
    return [
        jax.ShapeDtypeStruct((count, nope_width, latent_width), BF16),
        jax.ShapeDtypeStruct((count, latent_width, value_width), BF16),
    ]


def partial_scratch(paired, group, key_count, nope_width, latent_width):
    slices = 4 if paired else 1
    return [
        pltpu.VMEM((slices, latent_width // slices, key_count), BF16),
        pltpu.VMEM((slices, group * nope_width // slices, key_count), BF16),
    ]


def attend(paired, begin, count, weights, final, qt, go, key_up, value_up, bias, kn_own, va_own, parts, before):
    _, nope_width, latent_width = key_up.shape
    value_width = value_up.shape[2]
    key_count, query_count = bias.shape
    row_width = parts[0].shape[1]
    out = lambda *dims: jax.ShapeDtypeStruct(dims, BF16)
    shapes = [out(count, key_count, query_count), out(count, key_count, nope_width)]
    if weights:
        shapes += partial_shapes(paired, count, nope_width, latent_width, value_width)
    else:
        shapes += [out(key_count, count * value_width)]
    shapes += [out(*p.shape) for p in parts] if final else [jax.ShapeDtypeStruct((key_count, row_width), F32)]
    group = min(4, count) if paired else 1
    return pl.pallas_call(
        functools.partial(attend_kernel, paired, before is None, final, weights, len(parts), begin, count, latent_width),
        out_shape=shapes,
        scratch_shapes=partial_scratch(paired, group, key_count, nope_width, latent_width) if weights else [],
        compiler_params=params(14 if paired else 56),
        cost_estimate=cost(count * (400_000_000 if weights else 300_000_000), count * 500_000),
        name="attend",
    )(qt, go, key_up, value_up, bias, kn_own, va_own, *parts, *([] if before is None else [before]))


def weights_kernel(paired, parts, counts, begin, latent_width, qt_ref, *rest):
    chunk_refs, rest = rest[:2 * len(counts)], rest[2 * len(counts):]
    part_refs, outs, vt_ref, bp_ref = rest[:parts], rest[parts:-2], rest[-2], rest[-1]
    latent = jnp.concatenate([r[:, :latent_width] for r in part_refs], axis=0)
    turned_values(paired, latent, vt_ref)
    at = 0
    for n, count in enumerate(counts):
        ds_ref, gv_ref = chunk_refs[2 * n], chunk_refs[2 * n + 1]
        value_width = gv_ref.shape[1] // count
        group = min(4, count)
        for g in range(0, count, group):
            weight_group(
                paired, at, [qt_ref[begin + at + i, :value_width] for i in range(group)], [ds_ref[g + i] for i in range(group)],
                gv_ref[:, g * value_width:(g + group) * value_width], latent, vt_ref, bp_ref, outs,
            )
            at += group


def weight_partials(begin, qt, chunks, parts, nope_width, latent_width):
    counts = [ds.shape[0] for ds, _ in chunks]
    count, key_count = sum(counts), chunks[0][0].shape[1]
    return pl.pallas_call(
        functools.partial(weights_kernel, True, len(parts), counts, begin, latent_width),
        out_shape=partial_shapes(True, count, nope_width, latent_width, nope_width),
        scratch_shapes=partial_scratch(True, 4, key_count, nope_width, latent_width),
        compiler_params=params(14),
        cost_estimate=cost(count * WEIGHT_COST, count * 400_000),
        name="weight_partials",
    )(qt, *[x for chunk in chunks for x in chunk], *parts)


def query_kernel(counts, parts, *refs):
    rotary_refs, refs = refs[:parts], refs[parts:]
    nope_ref, rope_ref = refs[-2:]
    rotary = jnp.concatenate([r[...] for r in rotary_refs], axis=0)
    nope_width = nope_ref.shape[1]
    rotary = rotary[:, rotary.shape[1] - rope_ref.shape[1]:]
    heads = sum(counts)
    query_count = rope_ref.shape[2]
    head = 0
    for c, count in enumerate(counts):
        ds_ref, kn_ref = refs[2 * c], refs[2 * c + 1]
        for h in range(count):
            ds = ds_ref[h]
            nope_ref[pl.ds(head, query_count, stride=heads), :] = dot_tn(ds, kn_ref[h])
            rope_ref[head] = dot_tn(rotary, ds)
            head += 1


def query_gradient(pairs, parts, rope_width):
    counts = [ds.shape[0] for ds, _ in pairs]
    heads = sum(counts)
    query_count, nope_width = pairs[0][0].shape[2], pairs[0][1].shape[2]
    nope, rope = pl.pallas_call(
        functools.partial(query_kernel, counts, len(parts)),
        out_shape=[
            jax.ShapeDtypeStruct((query_count * heads, nope_width), F32),
            jax.ShapeDtypeStruct((heads, rope_width, query_count), F32),
        ],
        compiler_params=params(8),
        cost_estimate=pl.CostEstimate(flops=1_000_000_000, bytes_accessed=5_000_000, transcendentals=0),
        name="query_gradient",
    )(*parts, *[x for pair in pairs for x in pair])
    return nope.reshape(1, query_count, heads, nope_width), jnp.transpose(rope, (2, 0, 1))[None]


def finish_kernel(places, first, far_ref, *rest):
    sources, rest = rest[:2 * len(places)], rest[2 * len(places) + (0 if first else 2):]
    key_hbm, value_hbm, key_ref, value_ref, sems = rest
    rows, width = key_ref.shape[1], value_ref.shape[2]
    copies = []
    for n, (inner, count, at, begin) in enumerate(places):
        own_ref, near_ref = sources[2 * n], sources[2 * n + 1]
        step = math.gcd(count, 2)
        for g in range(0, count, step):
            for h in range(g, g + step):
                total = own_ref[inner + h].astype(F32) + near_ref[inner + h].astype(F32) + far_ref[at + h].astype(F32)
                for j in range(key_ref.shape[2] // width):
                    key_ref[at + h, :, j * width:(j + 1) * width] = total[0, j * rows:(j + 1) * rows]
                value_ref[at + h] = total[1]
            for source, target in ((key_ref, key_hbm), (value_ref, value_hbm)):
                copies.append(pltpu.make_async_copy(
                    source.at[at + g:at + g + step], target.at[begin + g:begin + g + step], sems.at[len(copies)]
                ))
                copies[-1].start()
    for copy in copies:
        copy.wait()


def finish(pieces, far, heads, before):
    total, _, depth, width = far.shape
    rows = depth // 4
    places = [(inner, count, at, begin) for _, _, inner, count, at, begin in pieces]
    moves = sum(2 * count // math.gcd(count, 2) for _, count, _, _ in places)
    vmem, hbm = pl.BlockSpec(memory_space=pltpu.VMEM), pl.BlockSpec(memory_space=pltpu.HBM)
    operands = [far] + [x for piece in pieces for x in piece[:2]]
    return pl.pallas_call(
        functools.partial(finish_kernel, places, not before),
        in_specs=[vmem] * len(operands) + [hbm] * len(before),
        out_specs=[hbm] * 2,
        out_shape=[
            jax.ShapeDtypeStruct((heads, rows, 4 * width), F32),
            jax.ShapeDtypeStruct((heads, depth, width), F32),
        ],
        scratch_shapes=[
            pltpu.VMEM((total, rows, 4 * width), F32),
            pltpu.VMEM((total, depth, width), F32),
            pltpu.SemaphoreType.DMA((moves,)),
        ],
        input_output_aliases={len(operands): 0, len(operands) + 1: 1} if before else {},
        compiler_params=params(8),
        cost_estimate=cost(1_000_000, 300_000 * total),
        name="finish",
    )(*operands, *before)


def swap(x, axis, size, bits):
    return lax.ppermute(x, axis, [(i, i ^ bits) for i in range(size)])


def after(x, arrays, which):
    for n in which:
        x, arrays[n] = lax.optimization_barrier((x, arrays[n]))
    return x


def on_device(
    sizes, query_nope, query_rope, query_pos, latent_cache, block_table, key_up, value_up, grad_out
):
    head_size, ctx_size, dp_size = sizes
    heads, nope_width, latent_width = key_up.shape
    value_width = value_up.shape[2]
    page_rows, row_width = latent_cache.shape[2:]
    paired = (
        ctx_size == 2 and dp_size == 2 and latent_width == 4 * value_width and nope_width == value_width
        and nope_width % 64 == 0 and value_width % 128 == 0 and heads % 16 == 0
    )
    own_rows = latent_cache[0].reshape(-1, row_width)
    if ctx_size == 2:
        parts = [own_rows, swap(own_rows, "ctx", 2, 1)]
    else:
        parts = [lax.all_gather(own_rows, "ctx", axis=0, tiled=True)]
    rope = jnp.transpose(query_rope[0], (1, 2, 0))
    if paired:
        qt, go, ku, vu, own, bias, kn_own, va_own = prepare(
            2, query_nope[0], rope, grad_out[0], key_up, value_up, own_rows, query_pos, block_table, page_rows
        )
        parts[0] = own
        plan = [(heads * n // 16, weights) for n, weights in PLAN]
    else:
        qt = jnp.concatenate([jnp.transpose(query_nope[0], (1, 2, 0)), rope], axis=1)
        go, ku, vu = jnp.swapaxes(grad_out[0], 0, 1), key_up, value_up
        if ctx_size == 2:
            first = lax.axis_index("ctx") == 0
            parts = [jnp.concatenate([jnp.where(first, parts[0], parts[1]), jnp.where(first, parts[1], parts[0])], axis=0)]
        slots = jnp.arange(block_table.shape[1], dtype=jnp.int32)
        logical = jnp.sum(jnp.where(block_table[0][None, :] == slots[:, None], slots[None, :], 0), axis=1)
        positions = (logical[:, None] * page_rows + jnp.arange(page_rows, dtype=jnp.int32)[None, :]).reshape(-1, 1)
        bias = jnp.where(positions <= query_pos, 0.0, -jnp.inf).astype(F32)
        latent = parts[0][:, :latent_width]
        kn_own = jnp.einsum("kl,hnl->khn", latent, key_up, preferred_element_type=F32).astype(BF16).reshape(latent.shape[0], -1)
        va_own = jnp.einsum("kl,hlv->khv", latent, value_up, preferred_element_type=F32).astype(BF16).reshape(latent.shape[0], -1)
        plan = [(1, True)] * heads
    pairs, partials, pieces, fars, nears, later, total = [], [], [], [], [], [], None

    def send(begin, made):
        n = len(nears)
        keep0, keep1, send0, send1 = made
        near1 = swap(send1, "dp", 2, 1)
        inner = 0
        for size in CUTS[n]:
            cut = slice(inner, inner + heads * size // 16)
            sums = (keep1[cut].astype(F32) + near1[cut].astype(F32)).astype(BF16)
            at = 0
            if n in JOIN:
                at = fars[-1].shape[0]
                sums = jnp.concatenate([fars.pop(), sums], axis=0)
            pieces.append((keep0, n, (inner, cut.stop - inner, at, begin + inner), len(fars)))
            fars.append(sums)
            inner = cut.stop
        nears.append(send0)

    begin = 0
    for n, (count, weights) in enumerate(plan):
        final = n == len(plan) - 1
        if paired and final and FRONT:
            total, *fars[:FRONT] = lax.optimization_barrier((total, *fars[:FRONT]))
        results = list(attend(
            paired, begin, count, weights, final, qt, go, ku, vu, bias, kn_own, va_own, parts, total,
        ))
        pairs.append((results[0], results[1]))
        ends = results[-len(parts):] if final else results[-1:]
        if not weights:
            later.append((begin, (results[0], results[2])))
        elif paired:
            send(begin, results[2:6])
        else:
            partials.append(results[2:4])
        total = ends[0]
        begin += count
    for group in GROUPS if paired else ():
        chunks = [later[n][1] for n in group]
        if LATE and group[-1] != len(later) - 1:
            ends[-1], chunks[-1] = lax.optimization_barrier((ends[-1], chunks[-1]))
        send(later[group[0]][0], weight_partials(later[group[0]][0], qt, chunks, parts, nope_width, latent_width))
    fars = [swap(x, "ctx", 2, 1) for x in fars]
    for n, send0 in enumerate(nears):
        if WAITS[n] is not None:
            send0, fars[WAITS[n]] = lax.optimization_barrier((send0, fars[WAITS[n]]))
        nears[n] = swap(send0, "dp", 2, 1)
    if paired:
        grad_nope, grad_rope = query_gradient(pairs, parts, query_rope.shape[3])
        mine, other = ends
        other = after(other, fars, FARS.get(0, ()))
        share = mine.astype(F32) + swap(other, "ctx", 2, 1).astype(F32)
    else:
        ds, kn = (jnp.concatenate(x, axis=0) for x in zip(*pairs))
        wk, wv = (jnp.concatenate(x, axis=0) for x in zip(*partials))
        grad_nope = jnp.einsum("hkq,hkn->qhn", ds, kn, preferred_element_type=F32)[None]
        rotary = parts[0][:, latent_width:]
        grad_rope = jnp.einsum("hkq,kr->qhr", ds, rotary, preferred_element_type=F32)[None]
        grad_key_map = lax.psum_scatter(wk, ("ctx", "dp"), scatter_dimension=1, tiled=True).astype(F32)
        grad_value_map = lax.psum_scatter(wv, ("ctx", "dp"), scatter_dimension=1, tiled=True).astype(F32)
        share = lax.psum_scatter(ends[0], "ctx", scatter_dimension=0, tiled=True).astype(F32)
    if head_size & (head_size - 1) == 0:
        bits, n = 1, 0
        while bits < head_size:
            rounded = share.astype(BF16)
            if paired:
                rounded = after(rounded, fars, FARS.get(n + 1, ()))
                rounded = after(rounded, nears, NEARS.get(n + 1, ()))
            got = swap(rounded, "head", head_size, bits | (bits >> 1) if bits >= 4 else bits)
            share = rounded.astype(F32) + got.astype(F32)
            bits, n = bits * 2, n + 1
    else:
        share = lax.psum(share.astype(BF16), "head").astype(F32)
    if paired:
        maps = ()
        for m, far in enumerate(fars):
            part = [(own0, nears[n], *place) for own0, n, place, to in pieces if to == m]
            maps = finish(part, far, heads, maps)
        grad_key_map, grad_value_map = maps
    return (
        grad_nope,
        grad_rope,
        share.reshape(latent_cache.shape),
        grad_key_map,
        grad_value_map,
    )


def solution(mesh):
    sizes = tuple(mesh.shape[axis] for axis in ("head", "ctx", "dp"))
    placed = (
        P("dp", "ctx", "head", None),
        P("dp", "ctx", "head", None),
        P("dp", "ctx"),
        P("dp", "ctx", None, None),
        P("dp", None),
        P("head", None, None),
        P("head", None, None),
        P("dp", "ctx", "head", None),
    )
    return jax.shard_map(
        functools.partial(on_device, sizes),
        mesh=mesh,
        in_specs=placed,
        out_specs=(
            P("dp", "ctx", "head", None),
            P("dp", "ctx", "head", None),
            P("dp", "ctx", None, None),
            P("head", ("ctx", "dp"), None),
            P("head", ("ctx", "dp"), None),
        ),
        check_vma=False,
    )
```

```python
import functools
import math

import jax
import jax.numpy as jnp
from jax import lax
from jax.experimental import pallas as pl
from jax.experimental.pallas import tpu as pltpu
from jax.sharding import PartitionSpec as P

softmax_scale = 192.0 ** (-0.5)
F32 = jnp.float32
BF16 = jnp.bfloat16
MIB = 1024 * 1024
PLAN = ((4, True), (4, False), (8, False))
CUTS = ((4,), (4,), (4,), (4,))
GROUPS = ((0,), (1,), (2,))
WAITS = (None, None, None, None)
FARS = {2: (0,)}
NEARS = {}
FRONT = 1
WEIGHT_COST = 100_000_000
ATTEND_COST = 300_000_000
JOIN = (2, 3)
LATE = True


def dot_nn(a, b):
    return lax.dot_general(a, b, (((1,), (0,)), ((), ())), preferred_element_type=F32)


def dot_nt(a, b):
    return lax.dot_general(a, b, (((1,), (1,)), ((), ())), preferred_element_type=F32)


def dot_tn(a, b):
    return lax.dot_general(a, b, (((0,), (0,)), ((), ())), preferred_element_type=F32)


def params(mib):
    return pltpu.CompilerParams(vmem_limit_bytes=mib * MIB)


def cost(flops, moved):
    return pl.CostEstimate(flops=flops, bytes_accessed=moved, transcendentals=0)


def prepare_kernel(
    parts, page_rows, nope_hbm, rope_hbm, go_hbm, ku_hbm, vu_hbm, own_hbm, pos_hbm, table_hbm,
    qt_ref, go_ref, ku_ref, vu_ref, own_ref, bias_ref, kn_ref, va_ref,
    nope_in, go_in, rows_ref, pos_ref, table_ref, sems,
):
    heads, nope_width, latent_width = ku_ref.shape
    value_width = vu_ref.shape[2]
    query_count = go_ref.shape[1]
    moves = (
        (nope_hbm, nope_in), (go_hbm, go_in), (own_hbm, own_ref), (ku_hbm, ku_ref), (vu_hbm, vu_ref),
        (rope_hbm, qt_ref.at[:, nope_width:, :]), (table_hbm, table_ref), (pos_hbm, pos_ref),
    )
    copies = [pltpu.make_async_copy(a, b, sems.at[i]) for i, (a, b) in enumerate(moves)]
    for copy in copies:
        copy.start()
    copies[0].wait()
    rows_ref[...] = nope_in[...].astype(F32).reshape(query_count * heads, nope_width)
    for h in range(heads):
        qt_ref[h, :nope_width] = jnp.transpose(rows_ref[pl.ds(h, query_count, stride=heads), :]).astype(BF16)
    copies[1].wait()
    rows_ref[...] = go_in[...].astype(F32).reshape(query_count * heads, nope_width)
    for h in range(heads):
        go_ref[h] = rows_ref[pl.ds(h, query_count, stride=heads), :].astype(BF16)
    copies[6].wait()
    copies[7].wait()
    blocks = table_ref.shape[1]
    row = lax.broadcasted_iota(jnp.int32, (page_rows, query_count), 0)
    part_blocks = blocks // parts
    for i in range(blocks):
        slot = jnp.bitwise_xor(lax.axis_index("ctx"), i // part_blocks) * part_blocks + i % part_blocks if parts == 2 else i
        logical = jnp.int32(0)
        for b in range(blocks):
            logical = logical + jnp.where(table_ref[0, b] == slot, b, 0)
        visible = row + logical * page_rows <= pos_ref[...]
        bias_ref[i * page_rows:(i + 1) * page_rows] = jnp.where(visible, 0.0, -jnp.inf)
    copies[2].wait()
    latent = own_ref[:, :latent_width]
    copies[3].wait()
    step = 2
    for h in range(0, heads, step):
        ku = ku_ref[h:h + step].reshape(step * nope_width, latent_width)
        kn_ref[:, h * nope_width:(h + step) * nope_width] = dot_nt(latent, ku).astype(BF16)
    copies[4].wait()
    for h in range(0, heads, step):
        vu = jnp.concatenate([vu_ref[h + i] for i in range(step)], axis=1)
        va_ref[:, h * value_width:(h + step) * value_width] = dot_nn(latent, vu).astype(BF16)
    copies[5].wait()


def prepare(parts, nope, rope, go, key_up, value_up, own, pos, table, page_rows):
    query_count, heads, nope_width = nope.shape
    value_width = go.shape[2]
    key_count = table.shape[1] * page_rows
    out = lambda *dims: jax.ShapeDtypeStruct(dims, BF16)
    hbm = pl.BlockSpec(memory_space=pltpu.HBM)
    return pl.pallas_call(
        functools.partial(prepare_kernel, parts, page_rows),
        in_specs=[hbm] * 8,
        out_specs=[pl.BlockSpec(memory_space=pltpu.VMEM)] * 8,
        out_shape=[
            out(heads, nope_width + rope.shape[1], query_count), out(heads, query_count, value_width),
            out(*key_up.shape), out(*value_up.shape), out(*own.shape),
            jax.ShapeDtypeStruct((key_count, query_count), F32),
            out(own.shape[0], heads * nope_width), out(own.shape[0], heads * value_width),
        ],
        scratch_shapes=[
            pltpu.VMEM((query_count, heads, nope_width), BF16),
            pltpu.VMEM((query_count, heads, value_width), BF16),
            pltpu.VMEM((query_count * heads, nope_width), F32),
            pltpu.VMEM((1, query_count), jnp.int32),
            pltpu.SMEM((1, table.shape[1]), jnp.int32),
            pltpu.SemaphoreType.DMA((8,)),
        ],
        compiler_params=params(16),
        cost_estimate=cost(600_000_000, 12_000_000),
        name="prepare",
    )(*(pltpu.with_memory_space_constraint(x, pltpu.HBM) for x in (nope, rope, go, key_up, value_up, own, pos, table)))


def turned_values(paired, latent, vt_ref):
    slices, depth = vt_ref.shape[:2]
    turned = jnp.transpose(latent.astype(F32)).astype(BF16)
    for s in range(slices):
        vt_ref[place_of(paired, s)] = turned[s * depth:(s + 1) * depth]


def place_of(paired, s):
    if not paired:
        return s
    return jnp.bitwise_xor(s % 2, lax.axis_index("dp")) * 2 + jnp.bitwise_xor(s // 2, lax.axis_index("ctx"))


def weight_group(paired, at, qt, ds, gv, latent, vt_ref, bp_ref, outs):
    slices = vt_ref.shape[0]
    nope_slice = bp_ref.shape[1] // len(ds)
    value_width = gv.shape[1] // len(ds)
    for h in range(len(ds)):
        b = dot_nt(qt[h], ds[h]).astype(BF16)
        for s in range(slices):
            bp_ref[place_of(paired, s), h * nope_slice:(h + 1) * nope_slice] = b[s * nope_slice:(s + 1) * nope_slice]
    for s in range(slices):
        value_part = dot_nn(vt_ref[s], gv).astype(BF16)
        key_part = dot_nn(bp_ref[s], latent).astype(BF16)
        for h in range(len(ds)):
            rows = key_part[h * nope_slice:(h + 1) * nope_slice]
            columns = value_part[:, h * value_width:(h + 1) * value_width]
            if paired:
                for j in range(latent.shape[1] // value_width):
                    outs[s][at + h, 0, j * nope_slice:(j + 1) * nope_slice] = rows[:, j * value_width:(j + 1) * value_width]
                outs[s][at + h, 1] = columns
            else:
                outs[0][at + h] = rows
                outs[1][at + h] = columns


def attend_kernel(paired, first, final, weights, parts, begin, count, latent_width, qt_ref, go_ref, ku_ref, vu_ref, bias_ref, kn_own, va_own, *rest):
    rest = list(rest)
    part_refs = [rest.pop(0) for _ in range(parts)]
    before_ref = None if first else rest.pop(0)
    ds_ref, kn_ref = rest.pop(0), rest.pop(0)
    gv_ref = None if weights else rest.pop(0)
    outs = [rest.pop(0) for _ in range(4 if paired else 2)] if weights else None
    total_refs = [rest.pop(0) for _ in range(parts if final else 1)]
    nope_width = ku_ref.shape[1]
    value_width = vu_ref.shape[2]
    latent = jnp.concatenate([r[:, :latent_width] for r in part_refs], axis=0)
    rotary = jnp.concatenate([r[:, latent_width:] for r in part_refs], axis=0)
    if weights:
        vt_ref, bp_ref = rest
        turned_values(paired, latent, vt_ref)
        group = bp_ref.shape[1] * bp_ref.shape[0] // nope_width
    else:
        group = min(4, count)
    if not first:
        total = before_ref[...]
        total_latent, total_rotary = total[:, :latent_width], total[:, latent_width:]
    def front(g):
        at = begin + g
        heads = range(at, at + group)
        ku = ku_ref[at:at + group].reshape(group * nope_width, latent_width)
        vu = jnp.concatenate([vu_ref[h] for h in heads], axis=1)
        kn, values = kn_own[:, at * nope_width:(at + group) * nope_width], va_own[:, at * value_width:(at + group) * value_width]
        if parts == 2:
            far = latent[latent.shape[0] // 2:]
            kn = jnp.concatenate([kn, dot_nt(far, ku).astype(BF16)], axis=0)
            values = jnp.concatenate([values, dot_nn(far, vu).astype(BF16)], axis=0)
        raw = []
        for i, h in enumerate(heads):
            kn_h = kn[:, i * nope_width:(i + 1) * nope_width]
            kn_ref[g + i] = kn_h
            raw.append((
                dot_nn(jnp.concatenate([kn_h, rotary], axis=1), qt_ref[h]),
                dot_nt(values[:, i * value_width:(i + 1) * value_width], go_ref[h]),
            ))
        return at, heads, ku, vu, raw

    ahead = front(0)
    for g in range(0, count, group):
        at, heads, ku, vu, raw = ahead
        if g + group < count:
            ahead = front(g + group)
        soft = []
        for scores, grad_probs in raw:
            scores = scores * softmax_scale + bias_ref[...]
            top = jnp.max(scores, axis=0, keepdims=True)
            weight = jnp.exp(scores - top)
            inverse = 1.0 / jnp.sum(weight, axis=0, keepdims=True)
            delta = jnp.sum(weight * grad_probs, axis=0, keepdims=True) * inverse
            probs = weight * inverse
            soft.append((probs.astype(BF16), (probs * ((grad_probs - delta) * softmax_scale)).astype(BF16)))
        gkn, gv = [], []
        rotary_sum = None
        for i, h in enumerate(heads):
            probs, ds = soft[i]
            ds_ref[g + i] = ds
            gk = dot_nt(ds, qt_ref[h])
            gkn.append(gk[:, :nope_width].astype(BF16))
            rotary_sum = gk[:, nope_width:] if rotary_sum is None else rotary_sum + gk[:, nope_width:]
            gv.append(dot_nn(probs, go_ref[h]).astype(BF16))
        gv = jnp.concatenate(gv, axis=1)
        latent_sum = dot_nn(jnp.concatenate(gkn, axis=1), ku) + dot_nt(gv, vu)
        if first and g == 0:
            total_latent, total_rotary = latent_sum, rotary_sum
        else:
            total_latent, total_rotary = total_latent + latent_sum, total_rotary + rotary_sum
        if weights:
            weight_group(paired, g, [qt_ref[h, :nope_width] for h in heads], [d for _, d in soft], gv, latent, vt_ref, bp_ref, outs)
        else:
            gv_ref[:, g * value_width:(g + group) * value_width] = gv
    start = 0
    for ref in total_refs:
        stop = start + ref.shape[0]
        ref[:, :latent_width] = total_latent[start:stop].astype(ref.dtype)
        ref[:, latent_width:] = total_rotary[start:stop].astype(ref.dtype)
        start = stop


def partial_shapes(paired, count, nope_width, latent_width, value_width):
    if paired:
        return [jax.ShapeDtypeStruct((count, 2, latent_width // 4, value_width), BF16)] * 4
    return [
        jax.ShapeDtypeStruct((count, nope_width, latent_width), BF16),
        jax.ShapeDtypeStruct((count, latent_width, value_width), BF16),
    ]


def partial_scratch(paired, group, key_count, nope_width, latent_width):
    slices = 4 if paired else 1
    return [
        pltpu.VMEM((slices, latent_width // slices, key_count), BF16),
        pltpu.VMEM((slices, group * nope_width // slices, key_count), BF16),
    ]


def attend(paired, begin, count, weights, final, qt, go, key_up, value_up, bias, kn_own, va_own, parts, before):
    _, nope_width, latent_width = key_up.shape
    value_width = value_up.shape[2]
    key_count, query_count = bias.shape
    row_width = parts[0].shape[1]
    out = lambda *dims: jax.ShapeDtypeStruct(dims, BF16)
    shapes = [out(count, key_count, query_count), out(count, key_count, nope_width)]
    if weights:
        shapes += partial_shapes(paired, count, nope_width, latent_width, value_width)
    else:
        shapes += [out(key_count, count * value_width)]
    shapes += [out(*p.shape) for p in parts] if final else [jax.ShapeDtypeStruct((key_count, row_width), F32)]
    group = min(4, count) if paired else 1
    return pl.pallas_call(
        functools.partial(attend_kernel, paired, before is None, final, weights, len(parts), begin, count, latent_width),
        out_shape=shapes,
        scratch_shapes=partial_scratch(paired, group, key_count, nope_width, latent_width) if weights else [],
        compiler_params=params(14 if paired else 56),
        cost_estimate=cost(count * (400_000_000 if weights else ATTEND_COST), count * 500_000),
        name="attend",
    )(qt, go, key_up, value_up, bias, kn_own, va_own, *parts, *([] if before is None else [before]))


def weights_kernel(paired, parts, spans, begin, latent_width, qt_ref, *rest):
    chunk_refs, rest = rest[:2 * len(spans)], rest[2 * len(spans):]
    part_refs, outs, vt_ref, bp_ref = rest[:parts], rest[parts:-2], rest[-2], rest[-1]
    latent = jnp.concatenate([r[:, :latent_width] for r in part_refs], axis=0)
    turned_values(paired, latent, vt_ref)
    at = 0
    for n, (first, count) in enumerate(spans):
        ds_ref, gv_ref = chunk_refs[2 * n], chunk_refs[2 * n + 1]
        value_width = gv_ref.shape[1] // ds_ref.shape[0]
        group = min(4, count)
        for g in range(first, first + count, group):
            weight_group(
                paired, at, [qt_ref[begin + at + i, :value_width] for i in range(group)], [ds_ref[g + i] for i in range(group)],
                gv_ref[:, g * value_width:(g + group) * value_width], latent, vt_ref, bp_ref, outs,
            )
            at += group


def weight_partials(begin, qt, chunks, spans, parts, nope_width, latent_width):
    count, key_count = sum(n for _, n in spans), chunks[0][0].shape[1]
    return pl.pallas_call(
        functools.partial(weights_kernel, True, len(parts), spans, begin, latent_width),
        out_shape=partial_shapes(True, count, nope_width, latent_width, nope_width),
        scratch_shapes=partial_scratch(True, 4, key_count, nope_width, latent_width),
        compiler_params=params(14),
        cost_estimate=cost(count * WEIGHT_COST, count * 400_000),
        name="weight_partials",
    )(qt, *[x for chunk in chunks for x in chunk], *parts)


def query_kernel(counts, parts, *refs):
    rotary_refs, refs = refs[:parts], refs[parts:]
    nope_ref, rope_ref = refs[-2:]
    rotary = jnp.concatenate([r[...] for r in rotary_refs], axis=0)
    nope_width = nope_ref.shape[1]
    rotary = rotary[:, rotary.shape[1] - rope_ref.shape[1]:]
    heads = sum(counts)
    query_count = rope_ref.shape[2]
    head = 0
    for c, count in enumerate(counts):
        ds_ref, kn_ref = refs[2 * c], refs[2 * c + 1]
        for h in range(count):
            ds = ds_ref[h]
            nope_ref[pl.ds(head, query_count, stride=heads), :] = dot_tn(ds, kn_ref[h])
            rope_ref[head] = dot_tn(rotary, ds)
            head += 1


def query_gradient(pairs, parts, rope_width):
    counts = [ds.shape[0] for ds, _ in pairs]
    heads = sum(counts)
    query_count, nope_width = pairs[0][0].shape[2], pairs[0][1].shape[2]
    nope, rope = pl.pallas_call(
        functools.partial(query_kernel, counts, len(parts)),
        out_shape=[
            jax.ShapeDtypeStruct((query_count * heads, nope_width), F32),
            jax.ShapeDtypeStruct((heads, rope_width, query_count), F32),
        ],
        compiler_params=params(8),
        cost_estimate=pl.CostEstimate(flops=1_000_000_000, bytes_accessed=5_000_000, transcendentals=0),
        name="query_gradient",
    )(*parts, *[x for pair in pairs for x in pair])
    return nope.reshape(1, query_count, heads, nope_width), jnp.transpose(rope, (2, 0, 1))[None]


def finish_kernel(places, first, far_ref, *rest):
    sources, rest = rest[:2 * len(places)], rest[2 * len(places) + (0 if first else 2):]
    key_hbm, value_hbm, key_ref, value_ref, sems = rest
    rows, width = key_ref.shape[1], value_ref.shape[2]
    copies = []
    for n, (inner, count, at, begin) in enumerate(places):
        own_ref, near_ref = sources[2 * n], sources[2 * n + 1]
        step = math.gcd(count, 2)
        for g in range(0, count, step):
            for h in range(g, g + step):
                total = own_ref[inner + h].astype(F32) + near_ref[inner + h].astype(F32) + far_ref[at + h].astype(F32)
                for j in range(key_ref.shape[2] // width):
                    key_ref[at + h, :, j * width:(j + 1) * width] = total[0, j * rows:(j + 1) * rows]
                value_ref[at + h] = total[1]
            for source, target in ((key_ref, key_hbm), (value_ref, value_hbm)):
                copies.append(pltpu.make_async_copy(
                    source.at[at + g:at + g + step], target.at[begin + g:begin + g + step], sems.at[len(copies)]
                ))
                copies[-1].start()
    for copy in copies:
        copy.wait()


def finish(pieces, far, heads, before):
    total, _, depth, width = far.shape
    rows = depth // 4
    places = [(inner, count, at, begin) for _, _, inner, count, at, begin in pieces]
    moves = sum(2 * count // math.gcd(count, 2) for _, count, _, _ in places)
    vmem, hbm = pl.BlockSpec(memory_space=pltpu.VMEM), pl.BlockSpec(memory_space=pltpu.HBM)
    operands = [far] + [x for piece in pieces for x in piece[:2]]
    return pl.pallas_call(
        functools.partial(finish_kernel, places, not before),
        in_specs=[vmem] * len(operands) + [hbm] * len(before),
        out_specs=[hbm] * 2,
        out_shape=[
            jax.ShapeDtypeStruct((heads, rows, 4 * width), F32),
            jax.ShapeDtypeStruct((heads, depth, width), F32),
        ],
        scratch_shapes=[
            pltpu.VMEM((total, rows, 4 * width), F32),
            pltpu.VMEM((total, depth, width), F32),
            pltpu.SemaphoreType.DMA((moves,)),
        ],
        input_output_aliases={len(operands): 0, len(operands) + 1: 1} if before else {},
        compiler_params=params(8),
        cost_estimate=cost(1_000_000, 300_000 * total),
        name="finish",
    )(*operands, *before)


def swap(x, axis, size, bits):
    return lax.ppermute(x, axis, [(i, i ^ bits) for i in range(size)])


def after(x, arrays, which):
    for n in which:
        x, arrays[n] = lax.optimization_barrier((x, arrays[n]))
    return x


def on_device(
    sizes, query_nope, query_rope, query_pos, latent_cache, block_table, key_up, value_up, grad_out
):
    head_size, ctx_size, dp_size = sizes
    heads, nope_width, latent_width = key_up.shape
    value_width = value_up.shape[2]
    page_rows, row_width = latent_cache.shape[2:]
    paired = (
        ctx_size == 2 and dp_size == 2 and latent_width == 4 * value_width and nope_width == value_width
        and nope_width % 64 == 0 and value_width % 128 == 0 and heads % 16 == 0
    )
    own_rows = latent_cache[0].reshape(-1, row_width)
    if ctx_size == 2:
        parts = [own_rows, swap(own_rows, "ctx", 2, 1)]
    else:
        parts = [lax.all_gather(own_rows, "ctx", axis=0, tiled=True)]
    rope = jnp.transpose(query_rope[0], (1, 2, 0))
    if paired:
        qt, go, ku, vu, own, bias, kn_own, va_own = prepare(
            2, query_nope[0], rope, grad_out[0], key_up, value_up, own_rows, query_pos, block_table, page_rows
        )
        parts[0] = own
        plan = [(heads * n // 16, weights) for n, weights in PLAN]
    else:
        qt = jnp.concatenate([jnp.transpose(query_nope[0], (1, 2, 0)), rope], axis=1)
        go, ku, vu = jnp.swapaxes(grad_out[0], 0, 1), key_up, value_up
        if ctx_size == 2:
            first = lax.axis_index("ctx") == 0
            parts = [jnp.concatenate([jnp.where(first, parts[0], parts[1]), jnp.where(first, parts[1], parts[0])], axis=0)]
        slots = jnp.arange(block_table.shape[1], dtype=jnp.int32)
        logical = jnp.sum(jnp.where(block_table[0][None, :] == slots[:, None], slots[None, :], 0), axis=1)
        positions = (logical[:, None] * page_rows + jnp.arange(page_rows, dtype=jnp.int32)[None, :]).reshape(-1, 1)
        bias = jnp.where(positions <= query_pos, 0.0, -jnp.inf).astype(F32)
        latent = parts[0][:, :latent_width]
        kn_own = jnp.einsum("kl,hnl->khn", latent, key_up, preferred_element_type=F32).astype(BF16).reshape(latent.shape[0], -1)
        va_own = jnp.einsum("kl,hlv->khv", latent, value_up, preferred_element_type=F32).astype(BF16).reshape(latent.shape[0], -1)
        plan = [(1, True)] * heads
    pairs, partials, pieces, fars, nears, later, total = [], [], [], [], [], [], None

    def send(begin, made):
        n = len(nears)
        keep0, keep1, send0, send1 = made
        near1 = swap(send1, "dp", 2, 1)
        inner = 0
        for size in CUTS[n]:
            cut = slice(inner, inner + heads * size // 16)
            sums = (keep1[cut].astype(F32) + near1[cut].astype(F32)).astype(BF16)
            at = 0
            if n in JOIN:
                at = fars[-1].shape[0]
                sums = jnp.concatenate([fars.pop(), sums], axis=0)
            pieces.append((keep0, n, (inner, cut.stop - inner, at, begin + inner), len(fars)))
            fars.append(sums)
            inner = cut.stop
        nears.append(send0)

    begin = 0
    for n, (count, weights) in enumerate(plan):
        final = n == len(plan) - 1
        if paired and final and FRONT:
            total, *fars[:FRONT] = lax.optimization_barrier((total, *fars[:FRONT]))
        results = list(attend(
            paired, begin, count, weights, final, qt, go, ku, vu, bias, kn_own, va_own, parts, total,
        ))
        pairs.append((results[0], results[1]))
        ends = results[-len(parts):] if final else results[-1:]
        if not weights:
            step = math.gcd(count, heads // 4)
            later += [(begin + at, final, (results[0], results[2]), (at, step)) for at in range(0, count, step)]
        elif paired:
            send(begin, results[2:6])
        else:
            partials.append(results[2:4])
        total = ends[0]
        begin += count
    for group in GROUPS if paired else ():
        chunks = [later[n][2] for n in group]
        if LATE and not later[group[-1]][1]:
            ends[-1], chunks[-1] = lax.optimization_barrier((ends[-1], chunks[-1]))
        spans = [later[n][3] for n in group]
        send(later[group[0]][0], weight_partials(later[group[0]][0], qt, chunks, spans, parts, nope_width, latent_width))
    fars = [swap(x, "ctx", 2, 1) for x in fars]
    for n, send0 in enumerate(nears):
        if WAITS[n] is not None:
            send0, fars[WAITS[n]] = lax.optimization_barrier((send0, fars[WAITS[n]]))
        nears[n] = swap(send0, "dp", 2, 1)
    if paired:
        grad_nope, grad_rope = query_gradient(pairs, parts, query_rope.shape[3])
        mine, other = ends
        other = after(other, fars, FARS.get(0, ()))
        share = mine.astype(F32) + swap(other, "ctx", 2, 1).astype(F32)
    else:
        ds, kn = (jnp.concatenate(x, axis=0) for x in zip(*pairs))
        wk, wv = (jnp.concatenate(x, axis=0) for x in zip(*partials))
        grad_nope = jnp.einsum("hkq,hkn->qhn", ds, kn, preferred_element_type=F32)[None]
        rotary = parts[0][:, latent_width:]
        grad_rope = jnp.einsum("hkq,kr->qhr", ds, rotary, preferred_element_type=F32)[None]
        grad_key_map = lax.psum_scatter(wk, ("ctx", "dp"), scatter_dimension=1, tiled=True).astype(F32)
        grad_value_map = lax.psum_scatter(wv, ("ctx", "dp"), scatter_dimension=1, tiled=True).astype(F32)
        share = lax.psum_scatter(ends[0], "ctx", scatter_dimension=0, tiled=True).astype(F32)
    if head_size & (head_size - 1) == 0:
        bits, n = 1, 0
        while bits < head_size:
            rounded = share.astype(BF16)
            if paired:
                rounded = after(rounded, fars, FARS.get(n + 1, ()))
                rounded = after(rounded, nears, NEARS.get(n + 1, ()))
            got = swap(rounded, "head", head_size, bits | (bits >> 1) if bits >= 4 else bits)
            share = rounded.astype(F32) + got.astype(F32)
            bits, n = bits * 2, n + 1
    else:
        share = lax.psum(share.astype(BF16), "head").astype(F32)
    if paired:
        maps = ()
        for m, far in enumerate(fars):
            part = [(own0, nears[n], *place) for own0, n, place, to in pieces if to == m]
            maps = finish(part, far, heads, maps)
        grad_key_map, grad_value_map = maps
    return (
        grad_nope,
        grad_rope,
        share.reshape(latent_cache.shape),
        grad_key_map,
        grad_value_map,
    )


def solution(mesh):
    sizes = tuple(mesh.shape[axis] for axis in ("head", "ctx", "dp"))
    placed = (
        P("dp", "ctx", "head", None),
        P("dp", "ctx", "head", None),
        P("dp", "ctx"),
        P("dp", "ctx", None, None),
        P("dp", None),
        P("head", None, None),
        P("head", None, None),
        P("dp", "ctx", "head", None),
    )
    return jax.shard_map(
        functools.partial(on_device, sizes),
        mesh=mesh,
        in_specs=placed,
        out_specs=(
            P("dp", "ctx", "head", None),
            P("dp", "ctx", "head", None),
            P("dp", "ctx", None, None),
            P("head", ("ctx", "dp"), None),
            P("head", ("ctx", "dp"), None),
        ),
        check_vma=False,
    )
```

```python
import functools
import math

import jax
import jax.numpy as jnp
from jax import lax
from jax.experimental import pallas as pl
from jax.experimental.pallas import tpu as pltpu
from jax.sharding import PartitionSpec as P

softmax_scale = 192.0 ** (-0.5)
F32 = jnp.float32
BF16 = jnp.bfloat16
MIB = 1024 * 1024
PLAN = ((4, True), (4, False), (8, False))
CUTS = ((4,), (4,), (4,), (4,))
GROUPS = ((0,), (1,), (2,))
WAITS = (None, None, None, None)
FARS = {2: (0,)}
NEARS = {}
FRONT = 1
WEIGHT_COST = 100_000_000
ATTEND_COST = 300_000_000
JOIN = (2, 3)
LATE = True


def dot_nn(a, b):
    return lax.dot_general(a, b, (((1,), (0,)), ((), ())), preferred_element_type=F32)


def dot_nt(a, b):
    return lax.dot_general(a, b, (((1,), (1,)), ((), ())), preferred_element_type=F32)


def dot_tn(a, b):
    return lax.dot_general(a, b, (((0,), (0,)), ((), ())), preferred_element_type=F32)


def params(mib):
    return pltpu.CompilerParams(vmem_limit_bytes=mib * MIB)


def cost(flops, moved):
    return pl.CostEstimate(flops=flops, bytes_accessed=moved, transcendentals=0)


def prepare_kernel(
    parts, page_rows, nope_hbm, rope_hbm, go_hbm, ku_hbm, vu_hbm, own_hbm, pos_hbm, table_hbm,
    qt_ref, go_ref, ku_ref, vu_ref, own_ref, bias_ref, kn_ref, va_ref,
    nope_in, go_in, rows_ref, pos_ref, table_ref, sems,
):
    heads, nope_width, latent_width = ku_ref.shape
    value_width = vu_ref.shape[2]
    query_count = go_ref.shape[1]
    moves = (
        (nope_hbm, nope_in), (go_hbm, go_in), (own_hbm, own_ref), (ku_hbm, ku_ref), (vu_hbm, vu_ref),
        (rope_hbm, qt_ref.at[:, nope_width:, :]), (table_hbm, table_ref), (pos_hbm, pos_ref),
    )
    copies = [pltpu.make_async_copy(a, b, sems.at[i]) for i, (a, b) in enumerate(moves)]
    for copy in copies:
        copy.start()
    copies[0].wait()
    rows_ref[...] = nope_in[...].astype(F32).reshape(query_count * heads, nope_width)
    for h in range(heads):
        qt_ref[h, :nope_width] = jnp.transpose(rows_ref[pl.ds(h, query_count, stride=heads), :]).astype(BF16)
    copies[1].wait()
    rows_ref[...] = go_in[...].astype(F32).reshape(query_count * heads, nope_width)
    for h in range(heads):
        go_ref[h] = rows_ref[pl.ds(h, query_count, stride=heads), :].astype(BF16)
    copies[6].wait()
    copies[7].wait()
    blocks = table_ref.shape[1]
    row = lax.broadcasted_iota(jnp.int32, (page_rows, query_count), 0)
    part_blocks = blocks // parts
    for i in range(blocks):
        slot = jnp.bitwise_xor(lax.axis_index("ctx"), i // part_blocks) * part_blocks + i % part_blocks if parts == 2 else i
        logical = jnp.int32(0)
        for b in range(blocks):
            logical = logical + jnp.where(table_ref[0, b] == slot, b, 0)
        visible = row + logical * page_rows <= pos_ref[...]
        bias_ref[i * page_rows:(i + 1) * page_rows] = jnp.where(visible, 0.0, -jnp.inf)
    copies[2].wait()
    latent = own_ref[:, :latent_width]
    copies[3].wait()
    step = 2
    for h in range(0, heads, step):
        ku = ku_ref[h:h + step].reshape(step * nope_width, latent_width)
        kn_ref[:, h * nope_width:(h + step) * nope_width] = dot_nt(latent, ku).astype(BF16)
    copies[4].wait()
    for h in range(0, heads, step):
        vu = jnp.concatenate([vu_ref[h + i] for i in range(step)], axis=1)
        va_ref[:, h * value_width:(h + step) * value_width] = dot_nn(latent, vu).astype(BF16)
    copies[5].wait()


def prepare(parts, nope, rope, go, key_up, value_up, own, pos, table, page_rows):
    query_count, heads, nope_width = nope.shape
    value_width = go.shape[2]
    key_count = table.shape[1] * page_rows
    out = lambda *dims: jax.ShapeDtypeStruct(dims, BF16)
    hbm = pl.BlockSpec(memory_space=pltpu.HBM)
    return pl.pallas_call(
        functools.partial(prepare_kernel, parts, page_rows),
        in_specs=[hbm] * 8,
        out_specs=[pl.BlockSpec(memory_space=pltpu.VMEM)] * 8,
        out_shape=[
            out(heads, nope_width + rope.shape[1], query_count), out(heads, query_count, value_width),
            out(*key_up.shape), out(*value_up.shape), out(*own.shape),
            jax.ShapeDtypeStruct((key_count, query_count), F32),
            out(own.shape[0], heads * nope_width), out(own.shape[0], heads * value_width),
        ],
        scratch_shapes=[
            pltpu.VMEM((query_count, heads, nope_width), BF16),
            pltpu.VMEM((query_count, heads, value_width), BF16),
            pltpu.VMEM((query_count * heads, nope_width), F32),
            pltpu.VMEM((1, query_count), jnp.int32),
            pltpu.SMEM((1, table.shape[1]), jnp.int32),
            pltpu.SemaphoreType.DMA((8,)),
        ],
        compiler_params=params(16),
        cost_estimate=cost(600_000_000, 12_000_000),
        name="prepare",
    )(*(pltpu.with_memory_space_constraint(x, pltpu.HBM) for x in (nope, rope, go, key_up, value_up, own, pos, table)))


def turned_values(paired, latent, vt_ref):
    slices, depth = vt_ref.shape[:2]
    turned = jnp.transpose(latent.astype(F32)).astype(BF16)
    for s in range(slices):
        vt_ref[place_of(paired, s)] = turned[s * depth:(s + 1) * depth]


def place_of(paired, s):
    if not paired:
        return s
    return jnp.bitwise_xor(s % 2, lax.axis_index("dp")) * 2 + jnp.bitwise_xor(s // 2, lax.axis_index("ctx"))


def weight_group(paired, at, qt, ds, gv, latent, vt_ref, bp_ref, outs):
    slices = vt_ref.shape[0]
    nope_slice = bp_ref.shape[1] // len(ds)
    value_width = gv.shape[1] // len(ds)
    for h in range(len(ds)):
        b = dot_nt(qt[h], ds[h]).astype(BF16)
        for s in range(slices):
            bp_ref[place_of(paired, s), h * nope_slice:(h + 1) * nope_slice] = b[s * nope_slice:(s + 1) * nope_slice]
    for s in range(slices):
        value_part = dot_nn(vt_ref[s], gv).astype(BF16)
        key_part = dot_nn(bp_ref[s], latent).astype(BF16)
        for h in range(len(ds)):
            rows = key_part[h * nope_slice:(h + 1) * nope_slice]
            columns = value_part[:, h * value_width:(h + 1) * value_width]
            if paired:
                for j in range(latent.shape[1] // value_width):
                    outs[s][at + h, 0, j * nope_slice:(j + 1) * nope_slice] = rows[:, j * value_width:(j + 1) * value_width]
                outs[s][at + h, 1] = columns
            else:
                outs[0][at + h] = rows
                outs[1][at + h] = columns


def attend_kernel(paired, first, final, weights, parts, begin, count, latent_width, qt_ref, go_ref, ku_ref, vu_ref, bias_ref, kn_own, va_own, *rest):
    rest = list(rest)
    part_refs = [rest.pop(0) for _ in range(parts)]
    before_ref = None if first else rest.pop(0)
    ds_ref, kn_ref = rest.pop(0), rest.pop(0)
    gv_ref = None if weights else rest.pop(0)
    outs = [rest.pop(0) for _ in range(4 if paired else 2)] if weights else None
    total_refs = [rest.pop(0) for _ in range(parts if final else 1)]
    nope_width = ku_ref.shape[1]
    value_width = vu_ref.shape[2]
    latent = jnp.concatenate([r[:, :latent_width] for r in part_refs], axis=0)
    rotary = jnp.concatenate([r[:, latent_width:] for r in part_refs], axis=0)
    if weights:
        vt_ref, bp_ref = rest
        turned_values(paired, latent, vt_ref)
        group = bp_ref.shape[1] * bp_ref.shape[0] // nope_width
    else:
        group = min(4, count)
    if not first:
        total = before_ref[...]
        total_latent, total_rotary = total[:, :latent_width], total[:, latent_width:]
    def front(g):
        at = begin + g
        heads = range(at, at + group)
        ku = ku_ref[at:at + group].reshape(group * nope_width, latent_width)
        vu = jnp.concatenate([vu_ref[h] for h in heads], axis=1)
        kn, values = kn_own[:, at * nope_width:(at + group) * nope_width], va_own[:, at * value_width:(at + group) * value_width]
        if parts == 2:
            far = latent[latent.shape[0] // 2:]
            kn = jnp.concatenate([kn, dot_nt(far, ku).astype(BF16)], axis=0)
            values = jnp.concatenate([values, dot_nn(far, vu).astype(BF16)], axis=0)
        raw = []
        for i, h in enumerate(heads):
            kn_h = kn[:, i * nope_width:(i + 1) * nope_width]
            kn_ref[g + i] = kn_h
            raw.append((
                dot_nn(jnp.concatenate([kn_h, rotary], axis=1), qt_ref[h]),
                dot_nt(values[:, i * value_width:(i + 1) * value_width], go_ref[h]),
            ))
        return at, heads, ku, vu, raw

    ahead = front(0)
    for g in range(0, count, group):
        at, heads, ku, vu, raw = ahead
        if g + group < count:
            ahead = front(g + group)
        soft = []
        for scores, grad_probs in raw:
            scores = scores * softmax_scale + bias_ref[...]
            top = jnp.max(scores, axis=0, keepdims=True)
            weight = jnp.exp(scores - top)
            inverse = 1.0 / jnp.sum(weight, axis=0, keepdims=True)
            delta = jnp.sum(weight * grad_probs, axis=0, keepdims=True) * inverse
            probs = weight * inverse
            soft.append((probs.astype(BF16), (probs * ((grad_probs - delta) * softmax_scale)).astype(BF16)))
        gkn, gv = [], []
        rotary_sum = None
        for i, h in enumerate(heads):
            probs, ds = soft[i]
            ds_ref[g + i] = ds
            gk = dot_nt(ds, qt_ref[h])
            gkn.append(gk[:, :nope_width].astype(BF16))
            rotary_sum = gk[:, nope_width:] if rotary_sum is None else rotary_sum + gk[:, nope_width:]
            gv.append(dot_nn(probs, go_ref[h]).astype(BF16))
        gv = jnp.concatenate(gv, axis=1)
        latent_sum = dot_nn(jnp.concatenate(gkn, axis=1), ku) + dot_nt(gv, vu)
        if first and g == 0:
            total_latent, total_rotary = latent_sum, rotary_sum
        else:
            total_latent, total_rotary = total_latent + latent_sum, total_rotary + rotary_sum
        if weights:
            weight_group(paired, g, [qt_ref[h, :nope_width] for h in heads], [d for _, d in soft], gv, latent, vt_ref, bp_ref, outs)
        else:
            gv_ref[:, g * value_width:(g + group) * value_width] = gv
    if paired and final:
        for n, ref in enumerate(total_refs):
            rows = total_latent.shape[0] // parts
            start, half = n * rows, rows // 2
            blocks = latent_width // 128
            for j in range(blocks):
                ref[j * rows:(j + 1) * rows] = total_latent[start:start + rows, j * 128:(j + 1) * 128].astype(ref.dtype)
            ref[blocks * rows:] = jnp.concatenate(
                [total_rotary[start:start + half], total_rotary[start + half:start + rows]], axis=1
            ).astype(ref.dtype)
        return
    start = 0
    for ref in total_refs:
        stop = start + ref.shape[0]
        ref[:, :latent_width] = total_latent[start:stop].astype(ref.dtype)
        ref[:, latent_width:] = total_rotary[start:stop].astype(ref.dtype)
        start = stop


def partial_shapes(paired, count, nope_width, latent_width, value_width):
    if paired:
        return [jax.ShapeDtypeStruct((count, 2, latent_width // 4, value_width), BF16)] * 4
    return [
        jax.ShapeDtypeStruct((count, nope_width, latent_width), BF16),
        jax.ShapeDtypeStruct((count, latent_width, value_width), BF16),
    ]


def partial_scratch(paired, group, key_count, nope_width, latent_width):
    slices = 4 if paired else 1
    return [
        pltpu.VMEM((slices, latent_width // slices, key_count), BF16),
        pltpu.VMEM((slices, group * nope_width // slices, key_count), BF16),
    ]


def attend(paired, begin, count, weights, final, qt, go, key_up, value_up, bias, kn_own, va_own, parts, before):
    _, nope_width, latent_width = key_up.shape
    value_width = value_up.shape[2]
    key_count, query_count = bias.shape
    row_width = parts[0].shape[1]
    out = lambda *dims: jax.ShapeDtypeStruct(dims, BF16)
    shapes = [out(count, key_count, query_count), out(count, key_count, nope_width)]
    if weights:
        shapes += partial_shapes(paired, count, nope_width, latent_width, value_width)
    else:
        shapes += [out(key_count, count * value_width)]
    packed = lambda p: (p.shape[0] * p.shape[1] // 128, 128) if paired else p.shape
    shapes += [out(*packed(p)) for p in parts] if final else [jax.ShapeDtypeStruct((key_count, row_width), F32)]
    group = min(4, count) if paired else 1
    return pl.pallas_call(
        functools.partial(attend_kernel, paired, before is None, final, weights, len(parts), begin, count, latent_width),
        out_shape=shapes,
        scratch_shapes=partial_scratch(paired, group, key_count, nope_width, latent_width) if weights else [],
        compiler_params=params(14 if paired else 56),
        cost_estimate=cost(count * (400_000_000 if weights else ATTEND_COST), count * 500_000),
        name="attend",
    )(qt, go, key_up, value_up, bias, kn_own, va_own, *parts, *([] if before is None else [before]))


def weights_kernel(paired, parts, spans, begin, latent_width, qt_ref, *rest):
    chunk_refs, rest = rest[:2 * len(spans)], rest[2 * len(spans):]
    part_refs, outs, vt_ref, bp_ref = rest[:parts], rest[parts:-2], rest[-2], rest[-1]
    latent = jnp.concatenate([r[:, :latent_width] for r in part_refs], axis=0)
    turned_values(paired, latent, vt_ref)
    at = 0
    for n, (first, count) in enumerate(spans):
        ds_ref, gv_ref = chunk_refs[2 * n], chunk_refs[2 * n + 1]
        value_width = gv_ref.shape[1] // ds_ref.shape[0]
        group = min(4, count)
        for g in range(first, first + count, group):
            weight_group(
                paired, at, [qt_ref[begin + at + i, :value_width] for i in range(group)], [ds_ref[g + i] for i in range(group)],
                gv_ref[:, g * value_width:(g + group) * value_width], latent, vt_ref, bp_ref, outs,
            )
            at += group


def weight_partials(begin, qt, chunks, spans, parts, nope_width, latent_width):
    count, key_count = sum(n for _, n in spans), chunks[0][0].shape[1]
    return pl.pallas_call(
        functools.partial(weights_kernel, True, len(parts), spans, begin, latent_width),
        out_shape=partial_shapes(True, count, nope_width, latent_width, nope_width),
        scratch_shapes=partial_scratch(True, 4, key_count, nope_width, latent_width),
        compiler_params=params(14),
        cost_estimate=cost(count * WEIGHT_COST, count * 400_000),
        name="weight_partials",
    )(qt, *[x for chunk in chunks for x in chunk], *parts)


def query_kernel(counts, parts, *refs):
    rotary_refs, refs = refs[:parts], refs[parts:]
    nope_ref, rope_ref = refs[-2:]
    rotary = jnp.concatenate([r[...] for r in rotary_refs], axis=0)
    nope_width = nope_ref.shape[1]
    rotary = rotary[:, rotary.shape[1] - rope_ref.shape[1]:]
    heads = sum(counts)
    query_count = rope_ref.shape[2]
    head = 0
    for c, count in enumerate(counts):
        ds_ref, kn_ref = refs[2 * c], refs[2 * c + 1]
        for h in range(count):
            ds = ds_ref[h]
            nope_ref[pl.ds(head, query_count, stride=heads), :] = dot_tn(ds, kn_ref[h])
            rope_ref[head] = dot_tn(rotary, ds)
            head += 1


def query_gradient(pairs, parts, rope_width):
    counts = [ds.shape[0] for ds, _ in pairs]
    heads = sum(counts)
    query_count, nope_width = pairs[0][0].shape[2], pairs[0][1].shape[2]
    nope, rope = pl.pallas_call(
        functools.partial(query_kernel, counts, len(parts)),
        out_shape=[
            jax.ShapeDtypeStruct((query_count * heads, nope_width), F32),
            jax.ShapeDtypeStruct((heads, rope_width, query_count), F32),
        ],
        compiler_params=params(8),
        cost_estimate=pl.CostEstimate(flops=1_000_000_000, bytes_accessed=5_000_000, transcendentals=0),
        name="query_gradient",
    )(*parts, *[x for pair in pairs for x in pair])
    return nope.reshape(1, query_count, heads, nope_width), jnp.transpose(rope, (2, 0, 1))[None]


def unpack_kernel(one_ref, two_ref, out_ref):
    total = one_ref[...].astype(F32) + two_ref[...].astype(F32)
    rows, half = out_ref.shape[0], out_ref.shape[0] // 2
    blocks = out_ref.shape[1] // 128
    for j in range(blocks):
        out_ref[:, j * 128:(j + 1) * 128] = total[j * rows:(j + 1) * rows]
    rope = out_ref.shape[1] - blocks * 128
    out_ref[:half, blocks * 128:] = total[blocks * rows:, :rope]
    out_ref[half:, blocks * 128:] = total[blocks * rows:, rope:]


def unpack(one, two, rows, row_width):
    return pl.pallas_call(
        unpack_kernel,
        out_shape=jax.ShapeDtypeStruct((rows, row_width), F32),
        compiler_params=params(8),
        cost_estimate=cost(1_000_000, 600_000),
        name="unpack",
    )(one, two)


def finish_kernel(places, first, far_ref, *rest):
    sources, rest = rest[:2 * len(places)], rest[2 * len(places) + (0 if first else 2):]
    key_hbm, value_hbm, key_ref, value_ref, sems = rest
    rows, width = key_ref.shape[1], value_ref.shape[2]
    copies = []
    for n, (inner, count, at, begin) in enumerate(places):
        own_ref, near_ref = sources[2 * n], sources[2 * n + 1]
        step = math.gcd(count, 2)
        for g in range(0, count, step):
            for h in range(g, g + step):
                total = own_ref[inner + h].astype(F32) + near_ref[inner + h].astype(F32) + far_ref[at + h].astype(F32)
                for j in range(key_ref.shape[2] // width):
                    key_ref[at + h, :, j * width:(j + 1) * width] = total[0, j * rows:(j + 1) * rows]
                value_ref[at + h] = total[1]
            for source, target in ((key_ref, key_hbm), (value_ref, value_hbm)):
                copies.append(pltpu.make_async_copy(
                    source.at[at + g:at + g + step], target.at[begin + g:begin + g + step], sems.at[len(copies)]
                ))
                copies[-1].start()
    for copy in copies:
        copy.wait()


def finish(pieces, far, heads, before):
    total, _, depth, width = far.shape
    rows = depth // 4
    places = [(inner, count, at, begin) for _, _, inner, count, at, begin in pieces]
    moves = sum(2 * count // math.gcd(count, 2) for _, count, _, _ in places)
    vmem, hbm = pl.BlockSpec(memory_space=pltpu.VMEM), pl.BlockSpec(memory_space=pltpu.HBM)
    operands = [far] + [x for piece in pieces for x in piece[:2]]
    return pl.pallas_call(
        functools.partial(finish_kernel, places, not before),
        in_specs=[vmem] * len(operands) + [hbm] * len(before),
        out_specs=[hbm] * 2,
        out_shape=[
            jax.ShapeDtypeStruct((heads, rows, 4 * width), F32),
            jax.ShapeDtypeStruct((heads, depth, width), F32),
        ],
        scratch_shapes=[
            pltpu.VMEM((total, rows, 4 * width), F32),
            pltpu.VMEM((total, depth, width), F32),
            pltpu.SemaphoreType.DMA((moves,)),
        ],
        input_output_aliases={len(operands): 0, len(operands) + 1: 1} if before else {},
        compiler_params=params(8),
        cost_estimate=cost(1_000_000, 300_000 * total),
        name="finish",
    )(*operands, *before)


def swap(x, axis, size, bits):
    return lax.ppermute(x, axis, [(i, i ^ bits) for i in range(size)])


def after(x, arrays, which):
    for n in which:
        x, arrays[n] = lax.optimization_barrier((x, arrays[n]))
    return x


def on_device(
    sizes, query_nope, query_rope, query_pos, latent_cache, block_table, key_up, value_up, grad_out
):
    head_size, ctx_size, dp_size = sizes
    heads, nope_width, latent_width = key_up.shape
    value_width = value_up.shape[2]
    page_rows, row_width = latent_cache.shape[2:]
    paired = (
        ctx_size == 2 and dp_size == 2 and latent_width == 4 * value_width and nope_width == value_width
        and nope_width % 64 == 0 and value_width % 128 == 0 and heads % 16 == 0
        and 2 * (row_width - latent_width) == 128 and head_size > 1 and head_size & (head_size - 1) == 0
    )
    own_rows = latent_cache[0].reshape(-1, row_width)
    if ctx_size == 2:
        parts = [own_rows, swap(own_rows, "ctx", 2, 1)]
    else:
        parts = [lax.all_gather(own_rows, "ctx", axis=0, tiled=True)]
    rope = jnp.transpose(query_rope[0], (1, 2, 0))
    if paired:
        qt, go, ku, vu, own, bias, kn_own, va_own = prepare(
            2, query_nope[0], rope, grad_out[0], key_up, value_up, own_rows, query_pos, block_table, page_rows
        )
        parts[0] = own
        plan = [(heads * n // 16, weights) for n, weights in PLAN]
    else:
        qt = jnp.concatenate([jnp.transpose(query_nope[0], (1, 2, 0)), rope], axis=1)
        go, ku, vu = jnp.swapaxes(grad_out[0], 0, 1), key_up, value_up
        if ctx_size == 2:
            first = lax.axis_index("ctx") == 0
            parts = [jnp.concatenate([jnp.where(first, parts[0], parts[1]), jnp.where(first, parts[1], parts[0])], axis=0)]
        slots = jnp.arange(block_table.shape[1], dtype=jnp.int32)
        logical = jnp.sum(jnp.where(block_table[0][None, :] == slots[:, None], slots[None, :], 0), axis=1)
        positions = (logical[:, None] * page_rows + jnp.arange(page_rows, dtype=jnp.int32)[None, :]).reshape(-1, 1)
        bias = jnp.where(positions <= query_pos, 0.0, -jnp.inf).astype(F32)
        latent = parts[0][:, :latent_width]
        kn_own = jnp.einsum("kl,hnl->khn", latent, key_up, preferred_element_type=F32).astype(BF16).reshape(latent.shape[0], -1)
        va_own = jnp.einsum("kl,hlv->khv", latent, value_up, preferred_element_type=F32).astype(BF16).reshape(latent.shape[0], -1)
        plan = [(1, True)] * heads
    pairs, partials, pieces, fars, nears, later, total = [], [], [], [], [], [], None

    def send(begin, made):
        n = len(nears)
        keep0, keep1, send0, send1 = made
        near1 = swap(send1, "dp", 2, 1)
        inner = 0
        for size in CUTS[n]:
            cut = slice(inner, inner + heads * size // 16)
            sums = (keep1[cut].astype(F32) + near1[cut].astype(F32)).astype(BF16)
            at = 0
            if n in JOIN:
                at = fars[-1].shape[0]
                sums = jnp.concatenate([fars.pop(), sums], axis=0)
            pieces.append((keep0, n, (inner, cut.stop - inner, at, begin + inner), len(fars)))
            fars.append(sums)
            inner = cut.stop
        nears.append(send0)

    begin = 0
    for n, (count, weights) in enumerate(plan):
        final = n == len(plan) - 1
        if paired and final and FRONT:
            total, *fars[:FRONT] = lax.optimization_barrier((total, *fars[:FRONT]))
        results = list(attend(
            paired, begin, count, weights, final, qt, go, ku, vu, bias, kn_own, va_own, parts, total,
        ))
        pairs.append((results[0], results[1]))
        ends = results[-len(parts):] if final else results[-1:]
        if not weights:
            step = math.gcd(count, heads // 4)
            later += [(begin + at, final, (results[0], results[2]), (at, step)) for at in range(0, count, step)]
        elif paired:
            send(begin, results[2:6])
        else:
            partials.append(results[2:4])
        total = ends[0]
        begin += count
    for group in GROUPS if paired else ():
        chunks = [later[n][2] for n in group]
        if LATE and not later[group[-1]][1]:
            ends[-1], chunks[-1] = lax.optimization_barrier((ends[-1], chunks[-1]))
        spans = [later[n][3] for n in group]
        send(later[group[0]][0], weight_partials(later[group[0]][0], qt, chunks, spans, parts, nope_width, latent_width))
    fars = [swap(x, "ctx", 2, 1) for x in fars]
    for n, send0 in enumerate(nears):
        if WAITS[n] is not None:
            send0, fars[WAITS[n]] = lax.optimization_barrier((send0, fars[WAITS[n]]))
        nears[n] = swap(send0, "dp", 2, 1)
    if paired:
        grad_nope, grad_rope = query_gradient(pairs, parts, query_rope.shape[3])
        mine, other = ends
        other = after(other, fars, FARS.get(0, ()))
        share = mine.astype(F32) + swap(other, "ctx", 2, 1).astype(F32)
    else:
        ds, kn = (jnp.concatenate(x, axis=0) for x in zip(*pairs))
        wk, wv = (jnp.concatenate(x, axis=0) for x in zip(*partials))
        grad_nope = jnp.einsum("hkq,hkn->qhn", ds, kn, preferred_element_type=F32)[None]
        rotary = parts[0][:, latent_width:]
        grad_rope = jnp.einsum("hkq,kr->qhr", ds, rotary, preferred_element_type=F32)[None]
        grad_key_map = lax.psum_scatter(wk, ("ctx", "dp"), scatter_dimension=1, tiled=True).astype(F32)
        grad_value_map = lax.psum_scatter(wv, ("ctx", "dp"), scatter_dimension=1, tiled=True).astype(F32)
        share = lax.psum_scatter(ends[0], "ctx", scatter_dimension=0, tiled=True).astype(F32)
    if head_size & (head_size - 1) == 0:
        bits, n = 1, 0
        while bits < head_size:
            rounded = share.astype(BF16)
            if paired:
                rounded = after(rounded, fars, FARS.get(n + 1, ()))
                rounded = after(rounded, nears, NEARS.get(n + 1, ()))
            got = swap(rounded, "head", head_size, bits | (bits >> 1) if bits >= 4 else bits)
            share = rounded.astype(F32) + got.astype(F32)
            bits, n = bits * 2, n + 1
        if paired:
            share = unpack(rounded, got, *own_rows.shape)
    else:
        share = lax.psum(share.astype(BF16), "head").astype(F32)
    if paired:
        maps = ()
        for m, far in enumerate(fars):
            part = [(own0, nears[n], *place) for own0, n, place, to in pieces if to == m]
            maps = finish(part, far, heads, maps)
        grad_key_map, grad_value_map = maps
    return (
        grad_nope,
        grad_rope,
        share.reshape(latent_cache.shape),
        grad_key_map,
        grad_value_map,
    )


def solution(mesh):
    sizes = tuple(mesh.shape[axis] for axis in ("head", "ctx", "dp"))
    placed = (
        P("dp", "ctx", "head", None),
        P("dp", "ctx", "head", None),
        P("dp", "ctx"),
        P("dp", "ctx", None, None),
        P("dp", None),
        P("head", None, None),
        P("head", None, None),
        P("dp", "ctx", "head", None),
    )
    return jax.shard_map(
        functools.partial(on_device, sizes),
        mesh=mesh,
        in_specs=placed,
        out_specs=(
            P("dp", "ctx", "head", None),
            P("dp", "ctx", "head", None),
            P("dp", "ctx", None, None),
            P("head", ("ctx", "dp"), None),
            P("head", ("ctx", "dp"), None),
        ),
        check_vma=False,
    )
```

```python
import functools
import math

import jax
import jax.numpy as jnp
from jax import lax
from jax.experimental import pallas as pl
from jax.experimental.pallas import tpu as pltpu
from jax.sharding import PartitionSpec as P

softmax_scale = 192.0 ** (-0.5)
F32 = jnp.float32
BF16 = jnp.bfloat16
MIB = 1024 * 1024
PLAN = ((4, True), (4, False), (8, False))
CUTS = ((4,), (4,), (4,), (4,))
GROUPS = ((0,), (1,), (2,))
WAITS = (None, None, None, None)
FARS = {2: (0,)}
NEARS = {}
FRONT = 1
WEIGHT_COST = 100_000_000
ATTEND_COST = 300_000_000
JOIN = (2, 3)
LATE = True


def dot_nn(a, b):
    return lax.dot_general(a, b, (((1,), (0,)), ((), ())), preferred_element_type=F32)


def dot_nt(a, b):
    return lax.dot_general(a, b, (((1,), (1,)), ((), ())), preferred_element_type=F32)


def dot_tn(a, b):
    return lax.dot_general(a, b, (((0,), (0,)), ((), ())), preferred_element_type=F32)


def params(mib):
    return pltpu.CompilerParams(vmem_limit_bytes=mib * MIB)


def cost(flops, moved):
    return pl.CostEstimate(flops=flops, bytes_accessed=moved, transcendentals=0)


def prepare_kernel(
    parts, page_rows, nope_hbm, rope_hbm, go_hbm, ku_hbm, vu_hbm, own_hbm, pos_hbm, table_hbm,
    qt_ref, go_ref, ku_ref, vu_ref, own_ref, bias_ref, kn_ref, va_ref,
    nope_in, go_in, rows_ref, pos_ref, table_ref, sems,
):
    heads, nope_width, latent_width = ku_ref.shape
    value_width = vu_ref.shape[2]
    query_count = go_ref.shape[1]
    moves = (
        (nope_hbm, nope_in), (go_hbm, go_in), (own_hbm, own_ref), (ku_hbm, ku_ref), (vu_hbm, vu_ref),
        (rope_hbm, qt_ref.at[:, nope_width:, :]), (table_hbm, table_ref), (pos_hbm, pos_ref),
    )
    copies = [pltpu.make_async_copy(a, b, sems.at[i]) for i, (a, b) in enumerate(moves)]
    for copy in copies:
        copy.start()
    copies[0].wait()
    rows_ref[...] = nope_in[...].astype(F32).reshape(query_count * heads, nope_width)
    for h in range(heads):
        qt_ref[h, :nope_width] = jnp.transpose(rows_ref[pl.ds(h, query_count, stride=heads), :]).astype(BF16)
    copies[1].wait()
    rows_ref[...] = go_in[...].astype(F32).reshape(query_count * heads, nope_width)
    for h in range(heads):
        go_ref[h] = rows_ref[pl.ds(h, query_count, stride=heads), :].astype(BF16)
    copies[6].wait()
    copies[7].wait()
    blocks = table_ref.shape[1]
    row = lax.broadcasted_iota(jnp.int32, (page_rows, query_count), 0)
    part_blocks = blocks // parts
    for i in range(blocks):
        slot = jnp.bitwise_xor(lax.axis_index("ctx"), i // part_blocks) * part_blocks + i % part_blocks if parts == 2 else i
        logical = jnp.int32(0)
        for b in range(blocks):
            logical = logical + jnp.where(table_ref[0, b] == slot, b, 0)
        visible = row + logical * page_rows <= pos_ref[...]
        bias_ref[i * page_rows:(i + 1) * page_rows] = jnp.where(visible, 0.0, -jnp.inf)
    copies[2].wait()
    latent = own_ref[:, :latent_width]
    copies[3].wait()
    step = 2
    for h in range(0, heads, step):
        ku = ku_ref[h:h + step].reshape(step * nope_width, latent_width)
        kn_ref[:, h * nope_width:(h + step) * nope_width] = dot_nt(latent, ku).astype(BF16)
    copies[4].wait()
    for h in range(0, heads, step):
        vu = jnp.concatenate([vu_ref[h + i] for i in range(step)], axis=1)
        va_ref[:, h * value_width:(h + step) * value_width] = dot_nn(latent, vu).astype(BF16)
    copies[5].wait()


def prepare(parts, nope, rope, go, key_up, value_up, own, pos, table, page_rows):
    query_count, heads, nope_width = nope.shape
    value_width = go.shape[2]
    key_count = table.shape[1] * page_rows
    out = lambda *dims: jax.ShapeDtypeStruct(dims, BF16)
    hbm = pl.BlockSpec(memory_space=pltpu.HBM)
    return pl.pallas_call(
        functools.partial(prepare_kernel, parts, page_rows),
        in_specs=[hbm] * 8,
        out_specs=[pl.BlockSpec(memory_space=pltpu.VMEM)] * 8,
        out_shape=[
            out(heads, nope_width + rope.shape[1], query_count), out(heads, query_count, value_width),
            out(*key_up.shape), out(*value_up.shape), out(*own.shape),
            jax.ShapeDtypeStruct((key_count, query_count), F32),
            out(own.shape[0], heads * nope_width), out(own.shape[0], heads * value_width),
        ],
        scratch_shapes=[
            pltpu.VMEM((query_count, heads, nope_width), BF16),
            pltpu.VMEM((query_count, heads, value_width), BF16),
            pltpu.VMEM((query_count * heads, nope_width), F32),
            pltpu.VMEM((1, query_count), jnp.int32),
            pltpu.SMEM((1, table.shape[1]), jnp.int32),
            pltpu.SemaphoreType.DMA((8,)),
        ],
        compiler_params=params(16),
        cost_estimate=cost(600_000_000, 12_000_000),
        name="prepare",
    )(*(pltpu.with_memory_space_constraint(x, pltpu.HBM) for x in (nope, rope, go, key_up, value_up, own, pos, table)))


def turned_values(paired, latent, vt_ref):
    slices, depth = vt_ref.shape[:2]
    turned = jnp.transpose(latent.astype(F32)).astype(BF16)
    for s in range(slices):
        vt_ref[place_of(paired, s)] = turned[s * depth:(s + 1) * depth]


def place_of(paired, s):
    if not paired:
        return s
    return jnp.bitwise_xor(s % 2, lax.axis_index("dp")) * 2 + jnp.bitwise_xor(s // 2, lax.axis_index("ctx"))


def weight_group(paired, at, qt, ds, gv, latent, vt_ref, bp_ref, outs):
    slices = vt_ref.shape[0]
    nope_slice = bp_ref.shape[1] // len(ds)
    value_width = gv.shape[1] // len(ds)
    for h in range(len(ds)):
        b = dot_nt(qt[h], ds[h]).astype(BF16)
        for s in range(slices):
            bp_ref[place_of(paired, s), h * nope_slice:(h + 1) * nope_slice] = b[s * nope_slice:(s + 1) * nope_slice]
    for s in range(slices):
        value_part = dot_nn(vt_ref[s], gv).astype(BF16)
        key_part = dot_nn(bp_ref[s], latent).astype(BF16)
        for h in range(len(ds)):
            rows = key_part[h * nope_slice:(h + 1) * nope_slice]
            columns = value_part[:, h * value_width:(h + 1) * value_width]
            if paired:
                for j in range(latent.shape[1] // value_width):
                    outs[s][at + h, 0, j * nope_slice:(j + 1) * nope_slice] = rows[:, j * value_width:(j + 1) * value_width]
                outs[s][at + h, 1] = columns
            else:
                outs[0][at + h] = rows
                outs[1][at + h] = columns


def attend_kernel(paired, first, final, weights, parts, begin, count, latent_width, qt_ref, go_ref, ku_ref, vu_ref, bias_ref, kn_own, va_own, *rest):
    rest = list(rest)
    part_refs = [rest.pop(0) for _ in range(parts)]
    before_ref = None if first else rest.pop(0)
    ds_ref, kn_ref = rest.pop(0), rest.pop(0)
    gv_ref = None if weights else rest.pop(0)
    outs = [rest.pop(0) for _ in range(4 if paired else 2)] if weights else None
    total_refs = [rest.pop(0) for _ in range(parts if final else 1)]
    nope_width = ku_ref.shape[1]
    value_width = vu_ref.shape[2]
    latent = jnp.concatenate([r[:, :latent_width] for r in part_refs], axis=0)
    rotary = jnp.concatenate([r[:, latent_width:] for r in part_refs], axis=0)
    if weights:
        vt_ref, bp_ref = rest
        turned_values(paired, latent, vt_ref)
        group = bp_ref.shape[1] * bp_ref.shape[0] // nope_width
    else:
        group = min(8, count)
    if not first:
        total = before_ref[...]
        total_latent, total_rotary = total[:, :latent_width], total[:, latent_width:]
    def front(g):
        at = begin + g
        heads = range(at, at + group)
        ku = ku_ref[at:at + group].reshape(group * nope_width, latent_width)
        vu = jnp.concatenate([vu_ref[h] for h in heads], axis=1)
        kn, values = kn_own[:, at * nope_width:(at + group) * nope_width], va_own[:, at * value_width:(at + group) * value_width]
        if parts == 2:
            far = latent[latent.shape[0] // 2:]
            kn = jnp.concatenate([kn, dot_nt(far, ku).astype(BF16)], axis=0)
            values = jnp.concatenate([values, dot_nn(far, vu).astype(BF16)], axis=0)
        raw = []
        for i, h in enumerate(heads):
            kn_h = kn[:, i * nope_width:(i + 1) * nope_width]
            kn_ref[g + i] = kn_h
            raw.append((
                dot_nn(jnp.concatenate([kn_h, rotary], axis=1), qt_ref[h]),
                dot_nt(values[:, i * value_width:(i + 1) * value_width], go_ref[h]),
            ))
        return at, heads, ku, vu, raw

    ahead = front(0)
    for g in range(0, count, group):
        at, heads, ku, vu, raw = ahead
        if g + group < count:
            ahead = front(g + group)
        soft = []
        for scores, grad_probs in raw:
            scores = scores * softmax_scale + bias_ref[...]
            top = jnp.max(scores, axis=0, keepdims=True)
            weight = jnp.exp(scores - top)
            inverse = 1.0 / jnp.sum(weight, axis=0, keepdims=True)
            delta = jnp.sum(weight * grad_probs, axis=0, keepdims=True) * inverse
            probs = weight * inverse
            soft.append((probs.astype(BF16), (probs * ((grad_probs - delta) * softmax_scale)).astype(BF16)))
        gkn, gv = [], []
        rotary_sum = None
        for i, h in enumerate(heads):
            probs, ds = soft[i]
            ds_ref[g + i] = ds
            gk = dot_nt(ds, qt_ref[h])
            gkn.append(gk[:, :nope_width].astype(BF16))
            rotary_sum = gk[:, nope_width:] if rotary_sum is None else rotary_sum + gk[:, nope_width:]
            gv.append(dot_nn(probs, go_ref[h]).astype(BF16))
        gv = jnp.concatenate(gv, axis=1)
        latent_sum = dot_nn(jnp.concatenate(gkn, axis=1), ku) + dot_nt(gv, vu)
        if first and g == 0:
            total_latent, total_rotary = latent_sum, rotary_sum
        else:
            total_latent, total_rotary = total_latent + latent_sum, total_rotary + rotary_sum
        if weights:
            weight_group(paired, g, [qt_ref[h, :nope_width] for h in heads], [d for _, d in soft], gv, latent, vt_ref, bp_ref, outs)
        else:
            gv_ref[:, g * value_width:(g + group) * value_width] = gv
    if paired and final:
        for n, ref in enumerate(total_refs):
            rows = total_latent.shape[0] // parts
            start, half = n * rows, rows // 2
            blocks = latent_width // 128
            for j in range(blocks):
                ref[j * rows:(j + 1) * rows] = total_latent[start:start + rows, j * 128:(j + 1) * 128].astype(ref.dtype)
            ref[blocks * rows:] = jnp.concatenate(
                [total_rotary[start:start + half], total_rotary[start + half:start + rows]], axis=1
            ).astype(ref.dtype)
        return
    start = 0
    for ref in total_refs:
        stop = start + ref.shape[0]
        ref[:, :latent_width] = total_latent[start:stop].astype(ref.dtype)
        ref[:, latent_width:] = total_rotary[start:stop].astype(ref.dtype)
        start = stop


def partial_shapes(paired, count, nope_width, latent_width, value_width):
    if paired:
        return [jax.ShapeDtypeStruct((count, 2, latent_width // 4, value_width), BF16)] * 4
    return [
        jax.ShapeDtypeStruct((count, nope_width, latent_width), BF16),
        jax.ShapeDtypeStruct((count, latent_width, value_width), BF16),
    ]


def partial_scratch(paired, group, key_count, nope_width, latent_width):
    slices = 4 if paired else 1
    return [
        pltpu.VMEM((slices, latent_width // slices, key_count), BF16),
        pltpu.VMEM((slices, group * nope_width // slices, key_count), BF16),
    ]


def attend(paired, begin, count, weights, final, qt, go, key_up, value_up, bias, kn_own, va_own, parts, before):
    _, nope_width, latent_width = key_up.shape
    value_width = value_up.shape[2]
    key_count, query_count = bias.shape
    row_width = parts[0].shape[1]
    out = lambda *dims: jax.ShapeDtypeStruct(dims, BF16)
    shapes = [out(count, key_count, query_count), out(count, key_count, nope_width)]
    if weights:
        shapes += partial_shapes(paired, count, nope_width, latent_width, value_width)
    else:
        shapes += [out(key_count, count * value_width)]
    packed = lambda p: (p.shape[0] * p.shape[1] // 128, 128) if paired else p.shape
    shapes += [out(*packed(p)) for p in parts] if final else [jax.ShapeDtypeStruct((key_count, row_width), F32)]
    group = min(4, count) if paired else 1
    return pl.pallas_call(
        functools.partial(attend_kernel, paired, before is None, final, weights, len(parts), begin, count, latent_width),
        out_shape=shapes,
        scratch_shapes=partial_scratch(paired, group, key_count, nope_width, latent_width) if weights else [],
        compiler_params=params(14 if paired else 56),
        cost_estimate=cost(count * (400_000_000 if weights else ATTEND_COST), count * 500_000),
        name="attend",
    )(qt, go, key_up, value_up, bias, kn_own, va_own, *parts, *([] if before is None else [before]))


def weights_kernel(paired, parts, spans, begin, latent_width, qt_ref, *rest):
    chunk_refs, rest = rest[:2 * len(spans)], rest[2 * len(spans):]
    part_refs, outs, vt_ref, bp_ref = rest[:parts], rest[parts:-2], rest[-2], rest[-1]
    latent = jnp.concatenate([r[:, :latent_width] for r in part_refs], axis=0)
    turned_values(paired, latent, vt_ref)
    at = 0
    for n, (first, count) in enumerate(spans):
        ds_ref, gv_ref = chunk_refs[2 * n], chunk_refs[2 * n + 1]
        value_width = gv_ref.shape[1] // ds_ref.shape[0]
        group = min(4, count)
        for g in range(first, first + count, group):
            weight_group(
                paired, at, [qt_ref[begin + at + i, :value_width] for i in range(group)], [ds_ref[g + i] for i in range(group)],
                gv_ref[:, g * value_width:(g + group) * value_width], latent, vt_ref, bp_ref, outs,
            )
            at += group


def weight_partials(begin, qt, chunks, spans, parts, nope_width, latent_width):
    count, key_count = sum(n for _, n in spans), chunks[0][0].shape[1]
    return pl.pallas_call(
        functools.partial(weights_kernel, True, len(parts), spans, begin, latent_width),
        out_shape=partial_shapes(True, count, nope_width, latent_width, nope_width),
        scratch_shapes=partial_scratch(True, 4, key_count, nope_width, latent_width),
        compiler_params=params(14),
        cost_estimate=cost(count * WEIGHT_COST, count * 400_000),
        name="weight_partials",
    )(qt, *[x for chunk in chunks for x in chunk], *parts)


def query_kernel(counts, parts, *refs):
    rotary_refs, refs = refs[:parts], refs[parts:]
    nope_ref, rope_ref = refs[-2:]
    rotary = jnp.concatenate([r[...] for r in rotary_refs], axis=0)
    nope_width = nope_ref.shape[1]
    rotary = rotary[:, rotary.shape[1] - rope_ref.shape[1]:]
    heads = sum(counts)
    query_count = rope_ref.shape[2]
    head = 0
    for c, count in enumerate(counts):
        ds_ref, kn_ref = refs[2 * c], refs[2 * c + 1]
        for h in range(count):
            ds = ds_ref[h]
            nope_ref[pl.ds(head, query_count, stride=heads), :] = dot_tn(ds, kn_ref[h])
            rope_ref[head] = dot_tn(rotary, ds)
            head += 1


def query_gradient(pairs, parts, rope_width):
    counts = [ds.shape[0] for ds, _ in pairs]
    heads = sum(counts)
    query_count, nope_width = pairs[0][0].shape[2], pairs[0][1].shape[2]
    nope, rope = pl.pallas_call(
        functools.partial(query_kernel, counts, len(parts)),
        out_shape=[
            jax.ShapeDtypeStruct((query_count * heads, nope_width), F32),
            jax.ShapeDtypeStruct((heads, rope_width, query_count), F32),
        ],
        compiler_params=params(8),
        cost_estimate=pl.CostEstimate(flops=1_000_000_000, bytes_accessed=5_000_000, transcendentals=0),
        name="query_gradient",
    )(*parts, *[x for pair in pairs for x in pair])
    return nope.reshape(1, query_count, heads, nope_width), jnp.transpose(rope, (2, 0, 1))[None]


def unpack_kernel(one_ref, two_ref, out_ref):
    total = one_ref[...].astype(F32) + two_ref[...].astype(F32)
    rows, half = out_ref.shape[0], out_ref.shape[0] // 2
    blocks = out_ref.shape[1] // 128
    for j in range(blocks):
        out_ref[:, j * 128:(j + 1) * 128] = total[j * rows:(j + 1) * rows]
    rope = out_ref.shape[1] - blocks * 128
    out_ref[:half, blocks * 128:] = total[blocks * rows:, :rope]
    out_ref[half:, blocks * 128:] = total[blocks * rows:, rope:]


def unpack(one, two, rows, row_width):
    return pl.pallas_call(
        unpack_kernel,
        out_shape=jax.ShapeDtypeStruct((rows, row_width), F32),
        compiler_params=params(8),
        cost_estimate=cost(1_000_000, 600_000),
        name="unpack",
    )(one, two)


def finish_kernel(places, first, far_ref, *rest):
    sources, rest = rest[:2 * len(places)], rest[2 * len(places) + (0 if first else 2):]
    key_hbm, value_hbm, key_ref, value_ref, sems = rest
    rows, width = key_ref.shape[1], value_ref.shape[2]
    copies = []
    for n, (inner, count, at, begin) in enumerate(places):
        own_ref, near_ref = sources[2 * n], sources[2 * n + 1]
        step = math.gcd(count, 2)
        for g in range(0, count, step):
            for h in range(g, g + step):
                total = own_ref[inner + h].astype(F32) + near_ref[inner + h].astype(F32) + far_ref[at + h].astype(F32)
                for j in range(key_ref.shape[2] // width):
                    key_ref[at + h, :, j * width:(j + 1) * width] = total[0, j * rows:(j + 1) * rows]
                value_ref[at + h] = total[1]
            for source, target in ((key_ref, key_hbm), (value_ref, value_hbm)):
                copies.append(pltpu.make_async_copy(
                    source.at[at + g:at + g + step], target.at[begin + g:begin + g + step], sems.at[len(copies)]
                ))
                copies[-1].start()
    for copy in copies:
        copy.wait()


def finish(pieces, far, heads, before):
    total, _, depth, width = far.shape
    rows = depth // 4
    places = [(inner, count, at, begin) for _, _, inner, count, at, begin in pieces]
    moves = sum(2 * count // math.gcd(count, 2) for _, count, _, _ in places)
    vmem, hbm = pl.BlockSpec(memory_space=pltpu.VMEM), pl.BlockSpec(memory_space=pltpu.HBM)
    operands = [far] + [x for piece in pieces for x in piece[:2]]
    return pl.pallas_call(
        functools.partial(finish_kernel, places, not before),
        in_specs=[vmem] * len(operands) + [hbm] * len(before),
        out_specs=[hbm] * 2,
        out_shape=[
            jax.ShapeDtypeStruct((heads, rows, 4 * width), F32),
            jax.ShapeDtypeStruct((heads, depth, width), F32),
        ],
        scratch_shapes=[
            pltpu.VMEM((total, rows, 4 * width), F32),
            pltpu.VMEM((total, depth, width), F32),
            pltpu.SemaphoreType.DMA((moves,)),
        ],
        input_output_aliases={len(operands): 0, len(operands) + 1: 1} if before else {},
        compiler_params=params(8),
        cost_estimate=cost(1_000_000, 300_000 * total),
        name="finish",
    )(*operands, *before)


def swap(x, axis, size, bits):
    return lax.ppermute(x, axis, [(i, i ^ bits) for i in range(size)])


def after(x, arrays, which):
    for n in which:
        x, arrays[n] = lax.optimization_barrier((x, arrays[n]))
    return x


def on_device(
    sizes, query_nope, query_rope, query_pos, latent_cache, block_table, key_up, value_up, grad_out
):
    head_size, ctx_size, dp_size = sizes
    heads, nope_width, latent_width = key_up.shape
    value_width = value_up.shape[2]
    page_rows, row_width = latent_cache.shape[2:]
    paired = (
        ctx_size == 2 and dp_size == 2 and latent_width == 4 * value_width and nope_width == value_width
        and nope_width % 64 == 0 and value_width % 128 == 0 and heads % 16 == 0
        and 2 * (row_width - latent_width) == 128 and head_size > 1 and head_size & (head_size - 1) == 0
    )
    own_rows = latent_cache[0].reshape(-1, row_width)
    if ctx_size == 2:
        parts = [own_rows, swap(own_rows, "ctx", 2, 1)]
    else:
        parts = [lax.all_gather(own_rows, "ctx", axis=0, tiled=True)]
    rope = jnp.transpose(query_rope[0], (1, 2, 0))
    if paired:
        qt, go, ku, vu, own, bias, kn_own, va_own = prepare(
            2, query_nope[0], rope, grad_out[0], key_up, value_up, own_rows, query_pos, block_table, page_rows
        )
        parts[0] = own
        plan = [(heads * n // 16, weights) for n, weights in PLAN]
    else:
        qt = jnp.concatenate([jnp.transpose(query_nope[0], (1, 2, 0)), rope], axis=1)
        go, ku, vu = jnp.swapaxes(grad_out[0], 0, 1), key_up, value_up
        if ctx_size == 2:
            first = lax.axis_index("ctx") == 0
            parts = [jnp.concatenate([jnp.where(first, parts[0], parts[1]), jnp.where(first, parts[1], parts[0])], axis=0)]
        slots = jnp.arange(block_table.shape[1], dtype=jnp.int32)
        logical = jnp.sum(jnp.where(block_table[0][None, :] == slots[:, None], slots[None, :], 0), axis=1)
        positions = (logical[:, None] * page_rows + jnp.arange(page_rows, dtype=jnp.int32)[None, :]).reshape(-1, 1)
        bias = jnp.where(positions <= query_pos, 0.0, -jnp.inf).astype(F32)
        latent = parts[0][:, :latent_width]
        kn_own = jnp.einsum("kl,hnl->khn", latent, key_up, preferred_element_type=F32).astype(BF16).reshape(latent.shape[0], -1)
        va_own = jnp.einsum("kl,hlv->khv", latent, value_up, preferred_element_type=F32).astype(BF16).reshape(latent.shape[0], -1)
        plan = [(1, True)] * heads
    pairs, partials, pieces, fars, nears, later, total = [], [], [], [], [], [], None

    def send(begin, made):
        n = len(nears)
        keep0, keep1, send0, send1 = made
        near1 = swap(send1, "dp", 2, 1)
        inner = 0
        for size in CUTS[n]:
            cut = slice(inner, inner + heads * size // 16)
            sums = (keep1[cut].astype(F32) + near1[cut].astype(F32)).astype(BF16)
            at = 0
            if n in JOIN:
                at = fars[-1].shape[0]
                sums = jnp.concatenate([fars.pop(), sums], axis=0)
            pieces.append((keep0, n, (inner, cut.stop - inner, at, begin + inner), len(fars)))
            fars.append(sums)
            inner = cut.stop
        nears.append(send0)

    begin = 0
    for n, (count, weights) in enumerate(plan):
        final = n == len(plan) - 1
        if paired and final and FRONT:
            total, *fars[:FRONT] = lax.optimization_barrier((total, *fars[:FRONT]))
        results = list(attend(
            paired, begin, count, weights, final, qt, go, ku, vu, bias, kn_own, va_own, parts, total,
        ))
        pairs.append((results[0], results[1]))
        ends = results[-len(parts):] if final else results[-1:]
        if not weights:
            step = math.gcd(count, heads // 4)
            later += [(begin + at, final, (results[0], results[2]), (at, step)) for at in range(0, count, step)]
        elif paired:
            send(begin, results[2:6])
        else:
            partials.append(results[2:4])
        total = ends[0]
        begin += count
    for group in GROUPS if paired else ():
        chunks = [later[n][2] for n in group]
        if LATE and not later[group[-1]][1]:
            ends[-1], chunks[-1] = lax.optimization_barrier((ends[-1], chunks[-1]))
        spans = [later[n][3] for n in group]
        send(later[group[0]][0], weight_partials(later[group[0]][0], qt, chunks, spans, parts, nope_width, latent_width))
    fars = [swap(x, "ctx", 2, 1) for x in fars]
    for n, send0 in enumerate(nears):
        if WAITS[n] is not None:
            send0, fars[WAITS[n]] = lax.optimization_barrier((send0, fars[WAITS[n]]))
        nears[n] = swap(send0, "dp", 2, 1)
    if paired:
        grad_nope, grad_rope = query_gradient(pairs, parts, query_rope.shape[3])
        mine, other = ends
        other = after(other, fars, FARS.get(0, ()))
        share = mine.astype(F32) + swap(other, "ctx", 2, 1).astype(F32)
    else:
        ds, kn = (jnp.concatenate(x, axis=0) for x in zip(*pairs))
        wk, wv = (jnp.concatenate(x, axis=0) for x in zip(*partials))
        grad_nope = jnp.einsum("hkq,hkn->qhn", ds, kn, preferred_element_type=F32)[None]
        rotary = parts[0][:, latent_width:]
        grad_rope = jnp.einsum("hkq,kr->qhr", ds, rotary, preferred_element_type=F32)[None]
        grad_key_map = lax.psum_scatter(wk, ("ctx", "dp"), scatter_dimension=1, tiled=True).astype(F32)
        grad_value_map = lax.psum_scatter(wv, ("ctx", "dp"), scatter_dimension=1, tiled=True).astype(F32)
        share = lax.psum_scatter(ends[0], "ctx", scatter_dimension=0, tiled=True).astype(F32)
    if head_size & (head_size - 1) == 0:
        bits, n = 1, 0
        while bits < head_size:
            rounded = share.astype(BF16)
            if paired:
                rounded = after(rounded, fars, FARS.get(n + 1, ()))
                rounded = after(rounded, nears, NEARS.get(n + 1, ()))
            got = swap(rounded, "head", head_size, bits | (bits >> 1) if bits >= 4 else bits)
            share = rounded.astype(F32) + got.astype(F32)
            bits, n = bits * 2, n + 1
        if paired:
            share = unpack(rounded, got, *own_rows.shape)
    else:
        share = lax.psum(share.astype(BF16), "head").astype(F32)
    if paired:
        maps = ()
        for m, far in enumerate(fars):
            part = [(own0, nears[n], *place) for own0, n, place, to in pieces if to == m]
            maps = finish(part, far, heads, maps)
        grad_key_map, grad_value_map = maps
    return (
        grad_nope,
        grad_rope,
        share.reshape(latent_cache.shape),
        grad_key_map,
        grad_value_map,
    )


def solution(mesh):
    sizes = tuple(mesh.shape[axis] for axis in ("head", "ctx", "dp"))
    placed = (
        P("dp", "ctx", "head", None),
        P("dp", "ctx", "head", None),
        P("dp", "ctx"),
        P("dp", "ctx", None, None),
        P("dp", None),
        P("head", None, None),
        P("head", None, None),
        P("dp", "ctx", "head", None),
    )
    return jax.shard_map(
        functools.partial(on_device, sizes),
        mesh=mesh,
        in_specs=placed,
        out_specs=(
            P("dp", "ctx", "head", None),
            P("dp", "ctx", "head", None),
            P("dp", "ctx", None, None),
            P("head", ("ctx", "dp"), None),
            P("head", ("ctx", "dp"), None),
        ),
        check_vma=False,
    )
```
